128 devices in a mesh: expert: 8 (over y, z_hi), tp: 16 (over x, z_lo, core).
Axes of the slice: x: 4, y: 4, z: 4 (z_hi: 2, z_lo: 2; z = z_hi * 2 + z_lo), core: 2. Of those that a mesh axis runs over, the one named last changes fastest.
Arguments:
- tokens: bfloat16 [2048, 3072], P(('expert', 'tp')), may hold values from -6 to 6
- routes: int32 [2048, 2], P(('expert', 'tp')), may hold values from 0 to 7, as said below
- counts: int32 [8], replicated, may hold values from 1 to 1536, as said below
- gate_weight: bfloat16 [8, 3072, 8192], P('expert', None, 'tp'), may hold values from -0.109375 to 0.109375
- up_weight: bfloat16 [8, 3072, 8192], P('expert', None, 'tp'), may hold values from -0.109375 to 0.109375
Outputs:
- hessian: float32 [8, 8192, 8192], P('expert', 'tp')
The draws below stay inside these ranges and needn't reach their ends.
Inputs may be any that keep to these rules, and one draw needn't show every extreme that they name: `routes`: each row names two different experts. Among the 16 rows of one device no expert is named by more than 12 rows, and the same expert is named by exactly 12 rows on every device. counts[e] is the number of rows of routes that name expert e.
All inputs are finite; a program needn't handle non-finite values.
Results may differ from the reference program's by a relative error of at most 0.004.
Values may be sent and summed in bfloat16 or wider, within the bound.
No kernel may reach another device: no remote copies, remote signals or barrier semaphores. Data moves between devices by JAX's collectives and lax.ppermute only.
A program may use at most 128 MiB of HBM per device.

```python
import jax
import jax.numpy as jnp
from jax import lax

D = 3072
FF = 8192
TOK_DEV = 16
EXPERTS = 8
SLOT = 12
TOKENS = 2048


def route_table(key):
    hot_expert = jax.random.randint(jax.random.fold_in(key, 11), (), 0, EXPERTS)
    blocks = TOKENS // TOK_DEV
    slot_count = 3 * TOK_DEV // 4
    spare_rows = TOK_DEV - slot_count
    others = EXPERTS - 1
    pool_size = others * slot_count
    taken = slot_count + 2 * spare_rows
    block_rank = jax.random.permutation(jax.random.fold_in(key, 12), blocks).astype(jnp.int32)
    second_shift = jax.random.randint(jax.random.fold_in(key, 14), (), 0, others)
    second = (block_rank + second_shift) % others
    coin = jax.random.randint(jax.random.fold_in(key, 15), (blocks,), 0, 2)
    forced = jnp.where(block_rank < others, 1, coin).astype(jnp.int32)
    pool_ids = (jnp.arange(pool_size, dtype=jnp.int32) // slot_count).astype(jnp.int32)
    pool_keys = jax.random.split(jax.random.fold_in(key, 16), blocks)
    shuffled = jax.vmap(lambda pool_key: jax.random.permutation(pool_key, pool_size))(pool_keys).astype(jnp.int32)
    drawn_ids = pool_ids[shuffled]
    favoured = jnp.logical_and(drawn_ids == second[:, None], forced[:, None] == 1).astype(jnp.int32)
    score = jnp.arange(pool_size, dtype=jnp.int32)[None, :] - pool_size * favoured
    order = jnp.argsort(score, axis=1, stable=True).astype(jnp.int32)
    picked = jnp.take_along_axis(drawn_ids, order, axis=1)[:, :taken]
    offsets = jnp.arange(others, dtype=jnp.int32)
    load = jnp.sum((picked[:, :, None] == offsets[None, None, :]).astype(jnp.int32), axis=1)
    run_keys = jax.random.split(jax.random.fold_in(key, 17), blocks)
    run_order = jax.vmap(lambda run_key: jax.random.permutation(run_key, others))(run_keys).astype(jnp.int32)
    run_length = jnp.take_along_axis(load, run_order, axis=1)
    run_end = jnp.cumsum(run_length, axis=1).astype(jnp.int32)
    places = jnp.arange(taken, dtype=jnp.int32)
    run_index = jnp.sum((run_end[:, None, :] <= places[None, :, None]).astype(jnp.int32), axis=2).astype(jnp.int32)
    other_offset = jnp.take_along_axis(run_order, run_index, axis=1)
    other_expert = (hot_expert + 1 + other_offset) % EXPERTS
    hot_part = jnp.full((blocks, slot_count), hot_expert, dtype=jnp.int32)
    table = jnp.concatenate([hot_part, other_expert.astype(jnp.int32)], axis=1)
    paired = jnp.stack([table[:, :TOK_DEV], table[:, TOK_DEV:]], axis=-1)
    block_keys = jax.random.split(jax.random.fold_in(key, 13), blocks)
    row_order = jax.vmap(lambda block_key: jax.random.permutation(block_key, TOK_DEV))(block_keys)
    paired = jnp.take_along_axis(paired, row_order[:, :, None].astype(jnp.int32), axis=1)
    routes = paired.reshape(TOKENS, 2).astype(jnp.int32)
    expert_ids = jnp.arange(EXPERTS, dtype=jnp.int32)
    counts = jnp.sum((routes[:, :, None] == expert_ids[None, None, :]).astype(jnp.int32), axis=(0, 1))
    return (routes, counts.astype(jnp.int32))


def draw_routes(key, part):
    routes, counts = route_table(key)
    return routes


def draw_counts(key, part):
    routes, counts = route_table(key)
    return counts


def levels(own_key, shape, pieces, low, top_value):
    factor_of = 1.0
    for axis_at, shards_of in pieces:
        steps = jax.random.uniform(jax.random.fold_in(jax.random.fold_in(own_key, 6), axis_at), (shards_of,), jnp.float32, low / len(pieces), top_value / len(pieces))
        factor_of = factor_of * jnp.repeat(jnp.exp(steps), shape[axis_at] // shards_of).reshape((-1,) + (1,) * (len(shape) - 1 - axis_at))
    return factor_of


def gaussian(rng, extent, deviation, limit, cuts=(), held_as=jnp.bfloat16):
    level = levels(rng, extent, cuts, -0.22, 0.18) if cuts else 1.0
    values = jax.random.normal(rng, extent, jnp.float32) * deviation * level
    return jnp.minimum(jnp.maximum(values, -limit), limit).astype(held_as)


def setup_inputs(seed: int = 0) -> dict:
    keys = jax.random.split(jax.random.key(seed), 6)
    tokens = gaussian(keys[0], (TOKENS, D), 1.0, 6.0, ((0, 128),))
    routes = draw_routes(jax.random.fold_in(keys[5], 71), 0)
    counts = draw_counts(jax.random.fold_in(keys[5], 71), 0)
    gate_weight = gaussian(keys[3], (EXPERTS, D, FF), D ** -0.5, 0.109375, ((0, 8), (2, 16)))
    up_weight = gaussian(keys[4], (EXPERTS, D, FF), D ** -0.5, 0.109375, ((0, 8), (2, 16)))
    return {"tokens": tokens, "routes": routes, "counts": counts, "gate_weight": gate_weight, "up_weight": up_weight}


def reference(tokens, routes, counts, gate_weight, up_weight):
    expert_ids = jnp.arange(EXPERTS, dtype=jnp.int32)

    def expert_gram(expert):
        routed = jnp.any(routes == expert, axis=1)
        row_order = jnp.argsort(jnp.where(routed, 0, 1).astype(jnp.int32), stable=True)[: SLOT * TOKENS // TOK_DEV]
        chosen = tokens[row_order] * routed[row_order][:, None].astype(tokens.dtype)
        gate_part = jnp.dot(chosen, gate_weight[expert], preferred_element_type=jnp.float32)
        up_part = jnp.dot(chosen, up_weight[expert], preferred_element_type=jnp.float32)
        hidden = (jax.nn.silu(gate_part) * up_part).astype(jnp.bfloat16)
        gram = lax.dot_general(hidden, hidden, (((0,), (0,)), ((), ())), preferred_element_type=jnp.float32)
        routed_total = jnp.sum(jnp.where(expert_ids == expert, counts, 0)).astype(jnp.float32)
        return gram * (2.0 / routed_total)

    return lax.map(expert_gram, expert_ids)
```

```python
import functools

import jax
import jax.numpy as jnp
from jax import lax
from jax.experimental import pallas as pl
from jax.experimental.pallas import tpu as pltpu
from jax.sharding import Mesh
from jax.sharding import PartitionSpec as P

AXES = ("y", "h", "x", "l", "c")
ROUTE_LANES = 128
VMEM_BYTES = 56 * 1024 * 1024
INTERPRET = False


def ring_hop(a, axis):
    pairs = [(2 * i + c, 2 * ((i + (1, 3)[c]) % 4) + c) for i in range(4) for c in range(2)]
    return lax.ppermute(a, (axis, "c"), pairs)


def swap(a, axis):
    return lax.ppermute(a, axis, [(0, 1), (1, 0)])


def far_swap(a):
    return lax.ppermute(a, ("h", "l"), [(0, 3), (3, 0), (1, 2), (2, 1)])


def ffn_kernel(slots, width, n, expert_ref, base_ref, wg_ref, wu_ref, *rest):
    sources = rest[: 2 * n]
    out_ref, held, rows, sems = rest[2 * n :]
    copies = [
        pltpu.make_async_copy(sources[i], held.at[i], sems.at[i]) for i in range(2 * n)
    ]
    for copy in copies:
        copy.start()
    tokens = held.shape[1]
    block_rows = rows.shape[0] // n
    expert = expert_ref[0].astype(jnp.float32)
    per_device = 16
    first = lax.broadcasted_iota(jnp.int32, (tokens, tokens), 0)
    second = lax.broadcasted_iota(jnp.int32, (tokens, tokens), 1)
    earlier = jnp.logical_and(first // per_device == second // per_device, first < second)
    earlier = earlier.astype(jnp.float32).astype(jnp.bfloat16)
    lane = lax.broadcasted_iota(jnp.int32, (tokens, ROUTE_LANES), 1)
    places = lax.broadcasted_iota(jnp.int32, (block_rows, tokens), 0).astype(jnp.float32)
    ones = jnp.ones((16, ROUTE_LANES), jnp.bfloat16)
    for i in range(n):
        total = None
        for part in range(2):
            j = 2 * i + part
            copies[j].wait()
            named = held[j, :, width:].astype(jnp.float32) == expert
            named = jnp.logical_and(named, lane < 2).astype(jnp.float32).astype(jnp.bfloat16)
            named = lax.dot_general(
                ones, named, (((1,), (1,)), ((), ())), preferred_element_type=jnp.float32
            )
            rank = jnp.dot(
                named.astype(jnp.bfloat16), earlier, preferred_element_type=jnp.float32
            )
            place = base_ref[j, 0:1, :] + rank[0:1, :]
            place = jnp.where(named[0:1, :] > 0.5, place, -1.0)
            pick = (places == place).astype(jnp.float32).astype(jnp.bfloat16)
            got = jnp.dot(pick, held[j, :, :width], preferred_element_type=jnp.float32)
            total = got if total is None else total + got
        rows[i * block_rows : (i + 1) * block_rows, :] = total.astype(jnp.bfloat16)
    gate = jnp.dot(rows[...], wg_ref[...], preferred_element_type=jnp.float32)
    up = jnp.dot(rows[...], wu_ref[...], preferred_element_type=jnp.float32)
    out_ref[...] = (gate / (1.0 + jnp.exp(-gate)) * up).astype(jnp.bfloat16)


def ffn(expert, arrivals, wg, wu):
    n = len(arrivals) // 2
    width, panel = wg.shape
    tokens = arrivals[0][0].shape[0]
    slots = 3 * 16 // 4
    block_rows = 2 * slots * tokens // 16
    bases = jnp.stack([b for _, b in arrivals])
    return pl.pallas_call(
        functools.partial(ffn_kernel, slots, width, n),
        out_shape=jax.ShapeDtypeStruct((n * block_rows, panel), jnp.bfloat16),
        in_specs=[
            pl.BlockSpec(memory_space=pltpu.SMEM),
            pl.BlockSpec(memory_space=pltpu.VMEM),
            pl.BlockSpec(memory_space=pltpu.VMEM),
            pl.BlockSpec(memory_space=pltpu.VMEM),
        ]
        + [pl.BlockSpec(memory_space=pl.ANY)] * (2 * n),
        out_specs=pl.BlockSpec(memory_space=pltpu.VMEM),
        scratch_shapes=[
            pltpu.VMEM((2 * n,) + arrivals[0][0].shape, jnp.bfloat16),
            pltpu.VMEM((n * block_rows, width), jnp.bfloat16),
            pltpu.SemaphoreType.DMA((2 * n,)),
        ],
        compiler_params=pltpu.CompilerParams(vmem_limit_bytes=VMEM_BYTES),
        cost_estimate=pl.CostEstimate(
            flops=4 * n * block_rows * width * panel, bytes_accessed=6_300_000, transcendentals=0
        ),
        interpret=INTERPRET,
    )(expert, bases, wg, wu, *[a for a, _ in arrivals])


def gram_kernel(counts_of, n_chunks, adding, ids_ref, scale_ref, *rest):
    n_sets = len(counts_of)
    own_refs = rest[:n_chunks]
    panel_refs = rest[n_chunks : n_chunks * (1 + n_sets)]
    old_ref = rest[n_chunks * (1 + n_sets)] if adding else None
    out_ref, turned = rest[-1 - n_chunks], rest[-n_chunks:]
    step = pl.program_id(0)

    @pl.when(step == 0)
    def _():
        for k in range(n_chunks):
            turned[k][...] = own_refs[k][...].T

    start = 0
    for s, count in enumerate(counts_of):

        @pl.when(jnp.logical_and(step >= start, step < start + count))
        def _(s=s):
            total = None
            for k in range(n_chunks):
                part = jnp.dot(
                    turned[k][...],
                    panel_refs[k * n_sets + s][0],
                    preferred_element_type=jnp.float32,
                )
                total = part if total is None else total + part
            total = total * scale_ref[0]
            out_ref[...] = total + old_ref[...] if adding else total

        start += count


def gram(ids, scale, owns, panels, features, old=None):
    counts_of = [p.shape[0] for p in panels[0]]
    panel = owns[0].shape[1]
    starts = [sum(counts_of[:s]) for s in range(len(counts_of))]
    specs, args = [], []
    for own in owns:
        specs.append(pl.BlockSpec(own.shape, lambda i, ids: (0, 0)))
        args.append(own)
    for sets in panels:
        for p, start in zip(sets, starts):
            specs.append(
                pl.BlockSpec(
                    (1,) + p.shape[1:],
                    lambda i, ids, start=start, n=p.shape[0]: (jnp.clip(i - start, 0, n - 1), 0, 0),
                )
            )
            args.append(p)
    out_spec = pl.BlockSpec((panel, panel), lambda i, ids: (0, ids[i]))
    if old is not None:
        specs.append(out_spec)
        args.append(old)
    return pl.pallas_call(
        functools.partial(gram_kernel, counts_of, len(owns), old is not None),
        out_shape=jax.ShapeDtypeStruct((panel, features), jnp.float32),
        grid_spec=pltpu.PrefetchScalarGridSpec(
            num_scalar_prefetch=1,
            grid=(sum(counts_of),),
            in_specs=[pl.BlockSpec(memory_space=pltpu.SMEM)] + specs,
            out_specs=out_spec,
            scratch_shapes=[pltpu.VMEM(own.shape[::-1], jnp.bfloat16) for own in owns],
        ),
        input_output_aliases={} if old is None else {1 + len(args): 0},
        compiler_params=pltpu.CompilerParams(vmem_limit_bytes=VMEM_BYTES),
        cost_estimate=pl.CostEstimate(
            flops=2 * sum(o.shape[0] for o in owns) * panel * panel * sum(counts_of),
            bytes_accessed=panel * panel * 4 * sum(counts_of),
            transcendentals=0,
        ),
        interpret=INTERPRET,
    )(ids, scale, *args)


def local(tokens, routes, counts, gate_weight, up_weight):
    x, l, c = lax.axis_index("x"), lax.axis_index("l"), lax.axis_index("c")
    expert = lax.axis_index("y") * 2 + lax.axis_index("h")
    gate_panel, up_panel = gate_weight[0], up_weight[0]
    panel = gate_panel.shape[1]
    features = 16 * panel
    routed_total = jnp.sum(jnp.where(jnp.arange(8) == expert, counts, 0)).astype(jnp.float32)
    scale = (2.0 / routed_total).reshape(1)
    expert = expert.reshape(1).astype(jnp.int32)

    def member(x_of, l_of, c_of):
        return (x_of % 4) * 4 + l_of * 2 + c_of

    tagged = jnp.concatenate(
        [tokens, jnp.pad(routes.astype(tokens.dtype), ((0, 0), (0, ROUTE_LANES - 2)))], axis=1
    )
    pair = jnp.stack([tagged, swap(tagged, "l")])
    quad = jnp.stack([pair, swap(pair, "c")])
    near = ring_hop(quad, "x")
    far = ring_hop(near[0], "x")
    other = swap(near, "c")
    mine = jnp.concatenate([quad[0], near[0], other[1], far])
    mine = mine.reshape((-1, mine.shape[-1]))

    def bases(l_of, c_of):
        s = 1 - 2 * c_of
        ids = [member(x_of, l_at, c_of) for x_of in (x, x - s, x + s, x + 2) for l_at in (l_of, 1 - l_of)]
        row = jnp.repeat(12 * jnp.stack(ids), 16).astype(jnp.float32)
        return jnp.broadcast_to(row, (8, 128))

    same = (bases(l, c), bases(l, 1 - c))
    flipped = (bases(1 - l, c), bases(1 - l, 1 - c))

    def arrival(block, base):
        return [(block, base[0]), (swap(block, "c"), base[1])]

    y1 = ring_hop(mine, "y")
    z0 = far_swap(mine)
    y2 = ring_hop(y1, "y")
    z1 = far_swap(y1)
    y3 = ring_hop(y2, "y")
    z2 = far_swap(y2)
    z3 = far_swap(y3)
    a0, a1 = arrival(mine, same), arrival(y1, same)
    a2, a3 = arrival(y2, same), arrival(y3, same)
    b0, b1 = arrival(z0, flipped), arrival(z1, flipped)
    b2, b3 = arrival(z2, flipped), arrival(z3, flipped)
    chunks = [a0 + a1, b0 + a2 + a3, b1 + b2, b3]

    s = 1 - 2 * c
    ids = (
        [member(x, l_at, c_at) for c_at in (c, 1 - c) for l_at in (l, 1 - l)]
        + [member(x - s, l_at, c_at) for c_at in (c, 1 - c) for l_at in (l, 1 - l)]
        + [member(x + s, l_at, c_at) for c_at in (1 - c, c) for l_at in (l, 1 - l)]
        + [member(x + 2, l_at, c_at) for c_at in (c, 1 - c) for l_at in (l, 1 - l)]
    )
    ids = jnp.stack(ids).astype(jnp.int32)

    owns, panels = [], []
    for chunk in chunks:
        hidden = ffn(expert, chunk, gate_panel, up_panel)
        h_pair = jnp.stack([hidden, swap(hidden, "l")])
        h_quad = jnp.concatenate([h_pair, swap(h_pair, "c")])
        h_near = ring_hop(h_quad, "x")
        h_far = ring_hop(h_near[:2], "x")
        owns.append(hidden)
        panels.append([h_quad, h_near, swap(h_near, "c"), h_far, swap(h_far, "c")])

    out = gram(ids, scale, owns[:2], panels[:2], features)
    out = gram(ids, scale, owns[2:3], panels[2:3], features, out)
    out = gram(ids[:12], scale, owns[3:], [panels[3][:3]], features, out)
    out = gram(ids[12:], scale, owns[3:], [panels[3][3:]], features, out)
    return out[None]


def solution(mesh):
    fine = Mesh(mesh.devices.reshape(4, 2, 4, 2, 2), AXES)
    rows = P(AXES, None)
    weight = P(("y", "h"), None, ("x", "l", "c"))
    return jax.shard_map(
        local,
        mesh=fine,
        in_specs=(rows, rows, P(), weight, weight),
        out_specs=P(("y", "h"), ("x", "l", "c"), None),
        check_vma=False,
    )
```

```python
import functools

import jax
import jax.numpy as jnp
from jax import lax
from jax.experimental import pallas as pl
from jax.experimental.pallas import tpu as pltpu
from jax.sharding import Mesh
from jax.sharding import PartitionSpec as P

AXES = ("y", "h", "x", "l", "c")
ROUTE_LANES = 128
VMEM_BYTES = 56 * 1024 * 1024
SLOTS = 12
INTERPRET = False
ANY = pl.BlockSpec(memory_space=pl.ANY)
SMEM = pl.BlockSpec(memory_space=pltpu.SMEM)
VMEM = pl.BlockSpec(memory_space=pltpu.VMEM)


def ring_hop(a, axis):
    pairs = [(2 * i + c, 2 * ((i + (1, 3)[c]) % 4) + c) for i in range(4) for c in range(2)]
    return lax.ppermute(a, (axis, "c"), pairs)


def ring_back(a, axis):
    pairs = [(2 * i + c, 2 * ((i + (3, 1)[c]) % 4) + c) for i in range(4) for c in range(2)]
    return lax.ppermute(a, (axis, "c"), pairs)


def swap(a, axis):
    return lax.ppermute(a, axis, [(0, 1), (1, 0)])


def far_swap(a):
    return lax.ppermute(a, ("h", "l"), [(0, 3), (3, 0), (1, 2), (2, 1)])


def after(a, *others):
    return lax.optimization_barrier((a,) + others)[0]


def tie(a, token):
    return lax.optimization_barrier((a, token))


def cost(microseconds):
    return pl.CostEstimate(
        flops=int(microseconds * 1_150_000_000), bytes_accessed=1_000_000, transcendentals=0
    )


def place_at(array, place):
    return array if place is None else array.at[place]


def select_kernel(n, width, expert_ref, base_ref, *rest):
    sources, (left_ref, right_ref, held, sems) = rest[:n], rest[n:]
    copies, row = [], 0
    for i, source in enumerate(sources):
        rows = pl.ds(row, source.shape[0])
        copies.append(pltpu.make_async_copy(source, held.at[rows], sems.at[i]))
        copies[-1].start()
        row += source.shape[0]
    tokens, out_rows = held.shape[0], left_ref.shape[0]
    first = lax.broadcasted_iota(jnp.int32, (tokens, tokens), 0)
    second = lax.broadcasted_iota(jnp.int32, (tokens, tokens), 1)
    earlier = jnp.logical_and(first // 16 == second // 16, first < second)
    earlier = earlier.astype(jnp.float32).astype(jnp.bfloat16)
    lane = lax.broadcasted_iota(jnp.int32, (tokens, ROUTE_LANES), 1)
    places = lax.broadcasted_iota(jnp.int32, (out_rows, tokens), 0).astype(jnp.float32)
    ones = jnp.ones((16, ROUTE_LANES), jnp.bfloat16)
    for copy in copies:
        copy.wait()
    named = held[:, width:].astype(jnp.float32) == expert_ref[0].astype(jnp.float32)
    named = jnp.logical_and(named, lane < 2).astype(jnp.float32).astype(jnp.bfloat16)
    named = lax.dot_general(
        ones, named, (((1,), (1,)), ((), ())), preferred_element_type=jnp.float32
    )
    rank = jnp.dot(named.astype(jnp.bfloat16), earlier, preferred_element_type=jnp.float32)
    place = jnp.where(named[0:1, :] > 0.5, base_ref[0:1, :] + rank[0:1, :], -1.0)
    pick = (places == place).astype(jnp.float32).astype(jnp.bfloat16)
    half = width // 2
    for out_ref, start in ((left_ref, 0), (right_ref, half)):
        got = jnp.dot(pick, held[:, start : start + half], preferred_element_type=jnp.float32)
        out_ref[...] = got.astype(jnp.bfloat16)


def select(expert, base, blocks, width):
    tokens = sum(b.shape[0] for b in blocks)
    half = jax.ShapeDtypeStruct((tokens // 16 * SLOTS, width // 2), jnp.bfloat16)
    return pl.pallas_call(
        functools.partial(select_kernel, len(blocks), width),
        out_shape=(half, half),
        in_specs=[SMEM, VMEM] + [ANY] * len(blocks),
        out_specs=(VMEM, VMEM),
        scratch_shapes=[
            pltpu.VMEM((tokens, blocks[0].shape[1]), jnp.bfloat16),
            pltpu.SemaphoreType.DMA((len(blocks),)),
        ],
        compiler_params=pltpu.CompilerParams(vmem_limit_bytes=VMEM_BYTES),
        cost_estimate=cost(3),
        interpret=INTERPRET,
    )(expert, base, *blocks)


def ffn_kernel(pieces, n_arrays, n_old, offsets_ref, *rest):
    arrays, (gate_hbm, up_hbm) = rest[:n_arrays], rest[n_arrays : n_arrays + 2]
    outs = rest[n_arrays + 2 + n_old : n_arrays + 4 + n_old]
    token_ref, rows, gate_held, up_held, result, sems, weight_sems, out_sems = rest[
        n_arrays + 4 + n_old :
    ]
    token_ref[...] = jnp.zeros_like(token_ref)
    piece_rows = rows.shape[0] // (len(pieces) // 2)
    width, half = rows.shape[1] // 2, gate_held.shape[1] // 2
    copies = []
    for i, (array, place) in enumerate(pieces):
        target = rows.at[
            pl.ds(i // 2 * piece_rows, piece_rows), pl.ds(i % 2 * width, width)
        ]
        copies.append(
            pltpu.make_async_copy(place_at(arrays[array], place), target, sems.at[i])
        )
    weight_copies = []
    for q in range(2):
        cols = pl.ds(q * half, half)
        for j, (src, dst) in enumerate(((gate_hbm, gate_held), (up_hbm, up_held))):
            weight_copies.append(
                pltpu.make_async_copy(src.at[:, cols], dst.at[:, cols], weight_sems.at[2 * q + j])
            )
    for copy in weight_copies[:2] + copies + weight_copies[2:]:
        copy.start()
    for copy in copies:
        copy.wait()
    sent = []
    for q in range(2):
        weight_copies[2 * q].wait()
        weight_copies[2 * q + 1].wait()
        cols = slice(q * half, (q + 1) * half)
        gate = jnp.dot(rows[...], gate_held[:, cols], preferred_element_type=jnp.float32)
        up = jnp.dot(rows[...], up_held[:, cols], preferred_element_type=jnp.float32)
        result[q] = (gate / (1.0 + jnp.exp(-gate)) * up).astype(jnp.bfloat16)
        for i in range(len(pieces) // 2):
            to = pl.ds(pl.multiple_of(offsets_ref[i], 16), piece_rows)
            sent.append(
                pltpu.make_async_copy(
                    result.at[q, pl.ds(i * piece_rows, piece_rows)],
                    outs[q].at[to],
                    out_sems.at[q, i],
                )
            )
            sent[-1].start()
    for copy in sent:
        copy.wait()


def ffn(offsets, pieces, wg, wu, total_rows, token, old=()):
    arrays, sources = [], []
    for array, place in pieces:
        at = [i for i, known in enumerate(arrays) if known is array]
        if not at:
            arrays.append(array)
            at = [len(arrays) - 1]
        sources.append((at[0], place))
    piece_rows = arrays[0].shape[-2]
    width, panel = wg.shape
    rows = len(pieces) // 2 * piece_rows
    out = jax.ShapeDtypeStruct((total_rows, panel // 2), jnp.bfloat16)
    first_old = 4 + len(arrays)
    return pl.pallas_call(
        functools.partial(ffn_kernel, sources, len(arrays), len(old) + 1),
        out_shape=(out, out, jax.ShapeDtypeStruct((8, 128), jnp.float32)),
        in_specs=[SMEM] + [ANY] * (len(arrays) + 3 + len(old)),
        out_specs=(ANY, ANY, VMEM),
        scratch_shapes=[
            pltpu.VMEM((rows, width), jnp.bfloat16),
            pltpu.VMEM(wg.shape, jnp.bfloat16),
            pltpu.VMEM(wu.shape, jnp.bfloat16),
            pltpu.VMEM((2, rows, panel // 2), jnp.bfloat16),
            pltpu.SemaphoreType.DMA((len(pieces),)),
            pltpu.SemaphoreType.DMA((4,)),
            pltpu.SemaphoreType.DMA((2, len(pieces) // 2)),
        ],
        input_output_aliases={first_old + i: i for i in range(len(old))},
        compiler_params=pltpu.CompilerParams(vmem_limit_bytes=VMEM_BYTES),
        cost_estimate=cost(1),
        interpret=INTERPRET,
    )(offsets, *arrays, wg, wu, token, *old)


def gram_kernel(sources, n_arrays, n_own, extra, ids_ref, scale_ref, *rest):
    own_refs, arrays = rest[:n_own], rest[n_own : n_own + n_arrays]
    out_ref, token_ref, *rest = rest[n_own + n_arrays + extra :]
    if n_own == 2:
        turned, own_held, held, result, own_sems, in_sems, out_sems = rest
    else:
        turned, held, result, own_sems, in_sems, out_sems = rest
    token_ref[...] = jnp.zeros_like(token_ref)
    half = held.shape[2]
    depth, count = held.shape[0], len(sources)

    def fetch(p):
        array, place = sources[p]
        copy = pltpu.make_async_copy(
            place_at(arrays[array], place), held.at[p % depth], in_sems.at[p % depth]
        )
        copy.start()
        return copy

    if n_own == 2:
        own = [
            pltpu.make_async_copy(own_refs[q], own_held.at[q], own_sems.at[q]) for q in range(2)
        ]
    else:
        own = [pltpu.make_async_copy(own_refs[0], turned, own_sems.at[0])]
    for copy in own:
        copy.start()
    fetched = {p: fetch(p) for p in range(min(depth, count))}
    for q, copy in enumerate(own):
        copy.wait()
        if n_own == 2:
            turned[q * half : (q + 1) * half, :] = own_held[q].T
    sent = {}
    for p in range(count):
        fetched[p].wait()
        total = jnp.dot(turned[...], held[p % depth], preferred_element_type=jnp.float32)
        if p >= 2:
            sent[p - 2].wait()
        result[p % 2] = total * scale_ref[0]
        if p + depth < count:
            fetched[p + depth] = fetch(p + depth)
        cols = pl.ds(pl.multiple_of(ids_ref[p] * half, half), half)
        sent[p] = pltpu.make_async_copy(result.at[p % 2], out_ref.at[:, cols], out_sems.at[p % 2])
        sent[p].start()
    for p in range(max(0, count - 2), count):
        sent[p].wait()


def gram(ids, scale, owns, panels, features, token, old=None):
    arrays, sources = [], []
    for array, place in panels:
        at = [i for i, known in enumerate(arrays) if known is array]
        if not at:
            arrays.append(array)
            at = [len(arrays) - 1]
        sources.append((at[0], place))
    rows, half = panels[0][0].shape[-2:]
    first = len(owns) == 2
    extra = 1 if old is None else 2
    turned = ((2 * half, rows), jnp.bfloat16)
    return pl.pallas_call(
        functools.partial(gram_kernel, sources, len(arrays), len(owns), extra),
        out_shape=(
            jax.ShapeDtypeStruct((2 * half, features), jnp.float32),
            jax.ShapeDtypeStruct((8, 128), jnp.float32),
        )
        + ((jax.ShapeDtypeStruct(*turned),) if first else ()),
        in_specs=[SMEM] * 2 + [ANY] * (len(owns) + len(arrays) + extra),
        out_specs=(ANY, VMEM) + ((VMEM,) if first else ()),
        scratch_shapes=[
            pltpu.VMEM((2, rows, half), jnp.bfloat16) if first else pltpu.VMEM(*turned),
            pltpu.VMEM((3, rows, half), jnp.bfloat16),
            pltpu.VMEM((2, 2 * half, half), jnp.float32),
            pltpu.SemaphoreType.DMA((2,)),
            pltpu.SemaphoreType.DMA((3,)),
            pltpu.SemaphoreType.DMA((2,)),
        ],
        input_output_aliases={} if old is None else {3 + len(owns) + len(arrays): 0},
        compiler_params=pltpu.CompilerParams(vmem_limit_bytes=VMEM_BYTES),
        cost_estimate=cost(1),
        interpret=INTERPRET,
    )(ids, scale, *owns, *arrays, token, *([] if old is None else [old]))


class Spread:
    def __init__(self):
        self.found = {}

    def keep(self, array, at, dl, side):
        twin = swap(array, "c")
        at_twin = {"o": "o", "m": "p", "f": "f"}[at]
        if array.ndim == 2:
            self.found[at, dl, 0, side] = (array, None)
            self.found[at_twin, dl, 1, side] = (twin, None)
        else:
            for half in (0, 1):
                self.found[at, dl, half, side] = (array, half)
                self.found[at_twin, dl, 1 - half, side] = (twin, half)
        return twin

    def first(self, left, right, token):
        beside, near_left = swap(right[0], "l"), ring_hop(left, "x")
        near_right, left_beside = ring_hop(right, "x"), swap(left[0], "l")
        left, right, *self.moved, token = lax.optimization_barrier(
            (left, right, beside, near_left, near_right, left_beside, token)
        )
        for half in (0, 1):
            self.found["o", 0, half, 0] = (left, half)
            self.found["o", 0, half, 1] = (right, half)
        return token

    def second(self):
        beside, near_left, near_right, left_beside = self.moved
        near_left_beside = swap(near_left, "l")
        far_left = ring_hop(near_left[0], "x")
        far_right = ring_hop(near_right[0], "x")
        twin = self.keep(beside, "o", 1, 1)
        near_beside = ring_hop(jnp.stack([beside, twin]), "x")
        self.keep(left_beside, "o", 1, 0)
        self.keep(near_left, "m", 0, 0)
        self.keep(near_right, "m", 0, 1)
        self.moved = (near_left_beside, far_left, far_right, near_beside)

    def third(self, token):
        near_left_beside, far_left, far_right, near_beside = self.moved
        far_left, token = tie(far_left, token)
        far_left_beside = swap(far_left, "l")
        near_left_beside, far_right, near_beside, token = lax.optimization_barrier(
            (near_left_beside, far_right, near_beside, token)
        )
        far_beside = ring_hop(near_beside[0], "x")
        self.keep(near_left_beside, "m", 1, 0)
        self.keep(near_beside, "m", 1, 1)
        self.keep(far_left, "f", 0, 0)
        self.keep(far_right, "f", 0, 1)
        self.moved = (far_left_beside, far_beside)
        return token

    def end(self, token):
        *moved, token = lax.optimization_barrier((*self.moved, token))
        self.keep(moved[0], "f", 1, 0)
        self.keep(moved[1], "f", 1, 1)
        return token


def local(tokens, routes, counts, gate_weight, up_weight):
    x, l, c = lax.axis_index("x"), lax.axis_index("l"), lax.axis_index("c")
    expert = lax.axis_index("y") * 2 + lax.axis_index("h")
    gate_panel, up_panel = gate_weight[0], up_weight[0]
    width, panel = gate_panel.shape
    features = 16 * panel
    routed_total = jnp.sum(jnp.where(jnp.arange(8) == expert, counts, 0)).astype(jnp.float32)
    scale = (2.0 / routed_total).reshape(1)
    expert = expert.reshape(1).astype(jnp.int32)

    tagged = jnp.concatenate(
        [tokens, jnp.pad(routes.astype(tokens.dtype), ((0, 0), (0, ROUTE_LANES - 2)))], axis=1
    )
    pair = jnp.stack([tagged, far_swap(tagged)])
    near, back = ring_hop(pair, "y"), ring_back(pair, "y")
    far = lax.ppermute(pair, "y", [(i, (i + 2) % 4) for i in range(4)])
    parts = [(a, swap(a, "c")) for a in (pair, near, back, far)]

    block = 8 * SLOTS
    y_near, y_back = 1 + c, 2 - c
    base = []
    for y_mine, y_twin in ((0, 0), (y_near, y_back), (y_back, y_near), (3, 3)):
        for dc, y_of in ((0, y_mine), (1, y_twin)):
            base += [dc * block + (2 * y_of + dh) * SLOTS for dh in (0, 1)]
    base = jnp.stack([jnp.asarray(b, jnp.int32) for b in base])
    base = jnp.broadcast_to(jnp.repeat(base, 16).astype(jnp.float32), (8, 256))
    blocks = [a.reshape((-1, a.shape[-1])) for part in parts for a in part]
    left, right = select(expert, base, blocks, width)

    place_of = {"o": x, "m": x - (1 - 2 * c), "p": x + (1 - 2 * c), "f": x + 2}

    def chip(at, dl):
        return (place_of[at] % 4) * 2 + (l + dl) % 2

    def offsets(chips):
        rows = [
            (chip(at, dl) * 2 + (c + half) % 2) * block for at, dl in chips for half in (0, 1)
        ]
        return jnp.stack(rows).astype(jnp.int32)

    def pieces(spread, chips):
        return [
            spread.found[at, dl, half, side] for at, dl in chips for half in (0, 1) for side in (0, 1)
        ]

    total = 16 * block

    def hidden_of(chips, token, *old):
        return ffn(offsets(chips), pieces(rows, chips), gate_panel, up_panel, total, token, old)

    token = jnp.zeros((8, 128), jnp.float32)
    rows = Spread()
    near = [("o", 0), ("o", 1), ("m", 0), ("p", 0)]
    beyond = [("m", 1), ("p", 1), ("f", 0)]
    last = [("f", 1)]
    token = rows.first(left.reshape(2, block, -1), right.reshape(2, block, -1), token)
    rows.second()
    *hidden, token = hidden_of(near, token)
    token = rows.third(token)
    *hidden, token = hidden_of(beyond, token, *hidden)
    token = rows.end(token)
    *hidden, token = hidden_of(last, token, *hidden)

    def columns(keys):
        ids = [(chip(at, dl) * 2 + (c + half) % 2) * 2 + side for at, dl, half, side in keys]
        return jnp.stack(ids).astype(jnp.int32)

    def part(chips, token, old=None):
        keys = [
            (at, dl, half, side) for at, dl in chips for side in (0, 1) for half in (0, 1)
        ]
        found = [panels.found[key] for key in keys]
        return gram(columns(keys), scale, own, found, features, token, old)

    panels = Spread()
    token = panels.first(*[jnp.stack([h, swap(h, "c")]) for h in hidden], token)
    panels.second()
    own = hidden
    out, token, *own = part(near, token)
    token = panels.third(token)
    out, token = part(beyond, token, out)
    token = panels.end(token)
    out, token = part(last, token, out)
    return out[None]


def solution(mesh):
    fine = Mesh(mesh.devices.reshape(4, 2, 4, 2, 2), AXES)
    rows = P(AXES, None)
    weight = P(("y", "h"), None, ("x", "l", "c"))
    return jax.shard_map(
        local,
        mesh=fine,
        in_specs=(rows, rows, P(), weight, weight),
        out_specs=P(("y", "h"), ("x", "l", "c"), None),
        check_vma=False,
    )
```

```python
import functools

import jax
import jax.numpy as jnp
from jax import lax
from jax.experimental import pallas as pl
from jax.experimental.pallas import tpu as pltpu
from jax.sharding import Mesh
from jax.sharding import PartitionSpec as P

AXES = ("y", "h", "x", "l", "c")
ROUTE_LANES = 128
VMEM_BYTES = 56 * 1024 * 1024
SLOTS = 12
INTERPRET = False
ANY = pl.BlockSpec(memory_space=pl.ANY)
SMEM = pl.BlockSpec(memory_space=pltpu.SMEM)
VMEM = pl.BlockSpec(memory_space=pltpu.VMEM)


def ring_hop(a, axis):
    pairs = [(2 * i + c, 2 * ((i + (1, 3)[c]) % 4) + c) for i in range(4) for c in range(2)]
    return lax.ppermute(a, (axis, "c"), pairs)


def ring_back(a, axis):
    pairs = [(2 * i + c, 2 * ((i + (3, 1)[c]) % 4) + c) for i in range(4) for c in range(2)]
    return lax.ppermute(a, (axis, "c"), pairs)


def swap(a, axis):
    return lax.ppermute(a, axis, [(0, 1), (1, 0)])


def far_swap(a):
    return lax.ppermute(a, ("h", "l"), [(0, 3), (3, 0), (1, 2), (2, 1)])


def after(a, *others):
    return lax.optimization_barrier((a,) + others)[0]


def tie(a, token):
    return lax.optimization_barrier((a, token))


def cost(microseconds):
    return pl.CostEstimate(
        flops=int(microseconds * 1_150_000_000), bytes_accessed=1_000_000, transcendentals=0
    )


def place_at(array, place):
    return array if place is None else array.at[place]


def select_kernel(n, width, expert_ref, base_ref, *rest):
    sources, (own_ref, twin_ref, held, sems) = rest[:n], rest[n:]
    copies, row = [], 0
    for i, source in enumerate(sources):
        rows = pl.ds(row, source.shape[0])
        copies.append(pltpu.make_async_copy(source, held.at[rows], sems.at[i]))
        copies[-1].start()
        row += source.shape[0]
    tokens, out_rows = held.shape[0], 2 * own_ref.shape[1]
    first = lax.broadcasted_iota(jnp.int32, (tokens, tokens), 0)
    second = lax.broadcasted_iota(jnp.int32, (tokens, tokens), 1)
    earlier = jnp.logical_and(first // 16 == second // 16, first < second)
    earlier = earlier.astype(jnp.float32).astype(jnp.bfloat16)
    lane = lax.broadcasted_iota(jnp.int32, (tokens, ROUTE_LANES), 1)
    places = lax.broadcasted_iota(jnp.int32, (out_rows, tokens), 0).astype(jnp.float32)
    ones = jnp.ones((16, ROUTE_LANES), jnp.bfloat16)
    for copy in copies:
        copy.wait()
    named = held[:, width:].astype(jnp.float32) == expert_ref[0].astype(jnp.float32)
    named = jnp.logical_and(named, lane < 2).astype(jnp.float32).astype(jnp.bfloat16)
    named = lax.dot_general(
        ones, named, (((1,), (1,)), ((), ())), preferred_element_type=jnp.float32
    )
    rank = jnp.dot(named.astype(jnp.bfloat16), earlier, preferred_element_type=jnp.float32)
    place = jnp.where(named[0:1, :] > 0.5, base_ref[0:1, :] + rank[0:1, :], -1.0)
    pick = (places == place).astype(jnp.float32).astype(jnp.bfloat16)
    half = width // 2
    for side, start in ((0, half), (1, 0)):
        got = jnp.dot(pick, held[:, start : start + half], preferred_element_type=jnp.float32)
        got = got.astype(jnp.bfloat16)
        own_ref[side] = got[: out_rows // 2]
        twin_ref[side] = got[out_rows // 2 :]


def select(expert, base, blocks, width):
    tokens = sum(b.shape[0] for b in blocks)
    half = jax.ShapeDtypeStruct((2, tokens // 32 * SLOTS, width // 2), jnp.bfloat16)
    return pl.pallas_call(
        functools.partial(select_kernel, len(blocks), width),
        out_shape=(half, half),
        in_specs=[SMEM, VMEM] + [ANY] * len(blocks),
        out_specs=(VMEM, VMEM),
        scratch_shapes=[
            pltpu.VMEM((tokens, blocks[0].shape[1]), jnp.bfloat16),
            pltpu.SemaphoreType.DMA((len(blocks),)),
        ],
        compiler_params=pltpu.CompilerParams(vmem_limit_bytes=VMEM_BYTES),
        cost_estimate=cost(3),
        interpret=INTERPRET,
    )(expert, base, *blocks)


def ffn_kernel(pieces, n_arrays, n_old, offsets_ref, *rest):
    arrays, (gate_hbm, up_hbm) = rest[:n_arrays], rest[n_arrays : n_arrays + 2]
    (
        out_ref,
        token_ref,
        rows,
        gate_held,
        up_held,
        result,
        sems,
        weight_sems,
        out_sems,
    ) = rest[n_arrays + 2 + n_old :]
    token_ref[...] = jnp.zeros_like(token_ref)
    piece_rows = rows.shape[0] // (len(pieces) // 2)
    width, half = rows.shape[1] // 2, gate_held.shape[1] // 2
    copies = []
    for i, (array, place) in enumerate(pieces):
        target = rows.at[
            pl.ds(i // 2 * piece_rows, piece_rows), pl.ds(i % 2 * width, width)
        ]
        copies.append(
            pltpu.make_async_copy(place_at(arrays[array], place), target, sems.at[i])
        )
    weight_copies = []
    for q in range(2):
        cols = pl.ds(q * half, half)
        for j, (src, dst) in enumerate(((gate_hbm, gate_held), (up_hbm, up_held))):
            weight_copies.append(
                pltpu.make_async_copy(src.at[:, cols], dst.at[:, cols], weight_sems.at[2 * q + j])
            )
    for copy in weight_copies[:2] + copies + weight_copies[2:]:
        copy.start()
    for copy in copies:
        copy.wait()
    sent = []
    for q in range(2):
        weight_copies[2 * q].wait()
        weight_copies[2 * q + 1].wait()
        cols = slice(q * half, (q + 1) * half)
        gate = jnp.dot(rows[...], gate_held[:, cols], preferred_element_type=jnp.float32)
        up = jnp.dot(rows[...], up_held[:, cols], preferred_element_type=jnp.float32)
        result[q] = (gate / (1.0 + jnp.exp(-gate)) * up).astype(jnp.bfloat16)
        for i in range(len(pieces) // 2):
            to = pl.ds(pl.multiple_of(offsets_ref[i], 16), piece_rows)
            sent.append(
                pltpu.make_async_copy(
                    result.at[q, pl.ds(i * piece_rows, piece_rows)],
                    out_ref.at[1 - q, to],
                    out_sems.at[q, i],
                )
            )
            sent[-1].start()
    for copy in sent:
        copy.wait()


def ffn(offsets, pieces, wg, wu, total_rows, token, old=()):
    arrays, sources = [], []
    for array, place in pieces:
        at = [i for i, known in enumerate(arrays) if known is array]
        if not at:
            arrays.append(array)
            at = [len(arrays) - 1]
        sources.append((at[0], place))
    piece_rows = arrays[0].shape[-2]
    width, panel = wg.shape
    rows = len(pieces) // 2 * piece_rows
    out = jax.ShapeDtypeStruct((2, total_rows, panel // 2), jnp.bfloat16)
    first_old = 4 + len(arrays)
    return pl.pallas_call(
        functools.partial(ffn_kernel, sources, len(arrays), len(old) + 1),
        out_shape=(out, jax.ShapeDtypeStruct((8, 128), jnp.float32)),
        in_specs=[SMEM] + [ANY] * (len(arrays) + 3 + len(old)),
        out_specs=(ANY, VMEM),
        scratch_shapes=[
            pltpu.VMEM((rows, width), jnp.bfloat16),
            pltpu.VMEM(wg.shape, jnp.bfloat16),
            pltpu.VMEM(wu.shape, jnp.bfloat16),
            pltpu.VMEM((2, rows, panel // 2), jnp.bfloat16),
            pltpu.SemaphoreType.DMA((len(pieces),)),
            pltpu.SemaphoreType.DMA((4,)),
            pltpu.SemaphoreType.DMA((2, len(pieces) // 2)),
        ],
        input_output_aliases={first_old + i: i for i in range(len(old))},
        compiler_params=pltpu.CompilerParams(vmem_limit_bytes=VMEM_BYTES),
        cost_estimate=cost(1),
        interpret=INTERPRET,
    )(offsets, *arrays, wg, wu, token, *old)


def gram_kernel(sources, n_arrays, first, extra, ids_ref, scale_ref, *rest):
    own_ref, *arrays = rest[: 1 + n_arrays]
    out_ref, token_ref, *rest = rest[1 + n_arrays + extra :]
    if first:
        turned, own_held, held, result, own_sems, in_sems, out_sems = rest
    else:
        turned, held, result, own_sems, in_sems, out_sems = rest
    token_ref[...] = jnp.zeros_like(token_ref)
    half = held.shape[2]
    depth, count = held.shape[0], len(sources)

    def fetch(p):
        array, place = sources[p]
        copy = pltpu.make_async_copy(
            place_at(arrays[array], place), held.at[p % depth], in_sems.at[p % depth]
        )
        copy.start()
        return copy

    if first:
        own = [
            pltpu.make_async_copy(own_ref.at[1 - q], own_held.at[q], own_sems.at[q])
            for q in range(2)
        ]
    else:
        own = [pltpu.make_async_copy(own_ref, turned, own_sems.at[0])]
    for copy in own:
        copy.start()
    fetched = {p: fetch(p) for p in range(min(depth, count))}
    for q, copy in enumerate(own):
        copy.wait()
        if first:
            turned[q * half : (q + 1) * half, :] = own_held[q].T
    sent = {}
    for p in range(count):
        fetched[p].wait()
        total = jnp.dot(turned[...], held[p % depth], preferred_element_type=jnp.float32)
        if p >= 2:
            sent[p - 2].wait()
        result[p % 2] = total * scale_ref[0]
        if p + depth < count:
            fetched[p + depth] = fetch(p + depth)
        cols = pl.ds(pl.multiple_of(ids_ref[p] * half, half), half)
        sent[p] = pltpu.make_async_copy(result.at[p % 2], out_ref.at[:, cols], out_sems.at[p % 2])
        sent[p].start()
    for p in range(max(0, count - 2), count):
        sent[p].wait()


def gram(ids, scale, own, panels, features, token, old=None):
    arrays, sources = [], []
    for array, place in panels:
        at = [i for i, known in enumerate(arrays) if known is array]
        if not at:
            arrays.append(array)
            at = [len(arrays) - 1]
        sources.append((at[0], place))
    rows, half = panels[0][0].shape[-2:]
    first = own.ndim == 3
    extra = 1 if old is None else 2
    turned = ((2 * half, rows), jnp.bfloat16)
    return pl.pallas_call(
        functools.partial(gram_kernel, sources, len(arrays), first, extra),
        out_shape=(
            jax.ShapeDtypeStruct((2 * half, features), jnp.float32),
            jax.ShapeDtypeStruct((8, 128), jnp.float32),
        )
        + ((jax.ShapeDtypeStruct(*turned),) if first else ()),
        in_specs=[SMEM] * 2 + [ANY] * (1 + len(arrays) + extra),
        out_specs=(ANY, VMEM) + ((VMEM,) if first else ()),
        scratch_shapes=[
            pltpu.VMEM((2, rows, half), jnp.bfloat16) if first else pltpu.VMEM(*turned),
            pltpu.VMEM((3, rows, half), jnp.bfloat16),
            pltpu.VMEM((2, 2 * half, half), jnp.float32),
            pltpu.SemaphoreType.DMA((2,)),
            pltpu.SemaphoreType.DMA((3,)),
            pltpu.SemaphoreType.DMA((2,)),
        ],
        input_output_aliases={} if old is None else {4 + len(arrays): 0},
        compiler_params=pltpu.CompilerParams(vmem_limit_bytes=VMEM_BYTES),
        cost_estimate=cost(1),
        interpret=INTERPRET,
    )(ids, scale, own, *arrays, token, *([] if old is None else [old]))


class Spread:
    def __init__(self):
        self.found = {}

    def keep(self, array, at, dl, keys):
        twin = swap(array, "c")
        at_twin = {"o": "o", "m": "p", "f": "f"}[at]
        for i, (half, side) in enumerate(keys):
            place = i if array.ndim == 3 else None
            self.found[at, dl, half, side] = (array, place)
            self.found[at_twin, dl, 1 - half, side] = (twin, place)
        return twin

    def open(self, pair, twin=None):
        beside, near = swap(pair, "l"), ring_hop(pair, "x")
        if twin is None:
            twin = swap(pair, "c")
        near_twin = ring_hop(twin, "x")
        for i, side in enumerate((1, 0)):
            self.found["o", 0, 0, side] = (pair, i)
            self.found["o", 0, 1, side] = (twin, i)
        self.moved = (beside, near, near_twin)

    def first(self, token):
        *self.moved, token = lax.optimization_barrier((*self.moved, token))
        return token

    def second(self):
        beside, near, near_twin = self.moved
        far = ring_hop(near, "x")
        left_beside = swap(jnp.stack([near[1], near_twin[1]]), "l")
        twin = self.keep(beside, "o", 1, ((0, 1), (0, 0)))
        right_beside = ring_hop(jnp.stack([beside[0], twin[0]]), "x")
        self.keep(near, "m", 0, ((0, 1), (0, 0)))
        self.keep(near_twin, "m", 0, ((1, 1), (1, 0)))
        self.moved = (far, left_beside, right_beside)

    def third(self, token):
        far, left_beside, right_beside = self.moved
        far, token = tie(far, token)
        far_left = swap(far[1], "l")
        left_beside, right_beside, token = lax.optimization_barrier(
            (left_beside, right_beside, token)
        )
        far_right = ring_hop(right_beside[0], "x")
        self.keep(left_beside, "m", 1, ((0, 0), (1, 0)))
        self.keep(right_beside, "m", 1, ((0, 1), (1, 1)))
        self.keep(far, "f", 0, ((0, 1), (0, 0)))
        self.moved = (far_left, far_right)
        return token

    def end(self, token):
        *moved, token = lax.optimization_barrier((*self.moved, token))
        self.keep(moved[0], "f", 1, ((0, 0),))
        self.keep(moved[1], "f", 1, ((0, 1),))
        return token


def local(tokens, routes, counts, gate_weight, up_weight):
    x, l, c = lax.axis_index("x"), lax.axis_index("l"), lax.axis_index("c")
    expert = lax.axis_index("y") * 2 + lax.axis_index("h")
    gate_panel, up_panel = gate_weight[0], up_weight[0]
    width, panel = gate_panel.shape
    features = 16 * panel
    routed_total = jnp.sum(jnp.where(jnp.arange(8) == expert, counts, 0)).astype(jnp.float32)
    scale = (2.0 / routed_total).reshape(1)
    expert = expert.reshape(1).astype(jnp.int32)

    tagged = jnp.concatenate(
        [tokens, jnp.pad(routes.astype(tokens.dtype), ((0, 0), (0, ROUTE_LANES - 2)))], axis=1
    )
    pair = jnp.stack([tagged, far_swap(tagged)])
    near, back = ring_hop(pair, "y"), ring_back(pair, "y")
    far = lax.ppermute(pair, "y", [(i, (i + 2) % 4) for i in range(4)])
    parts = [(a, swap(a, "c")) for a in (pair, near, back, far)]

    block = 8 * SLOTS
    y_near, y_back = 1 + c, 2 - c
    base = []
    for y_mine, y_twin in ((0, 0), (y_near, y_back), (y_back, y_near), (3, 3)):
        for dc, y_of in ((0, y_mine), (1, y_twin)):
            base += [dc * block + (2 * y_of + dh) * SLOTS for dh in (0, 1)]
    base = jnp.stack([jnp.asarray(b, jnp.int32) for b in base])
    base = jnp.broadcast_to(jnp.repeat(base, 16).astype(jnp.float32), (8, 256))
    blocks = [a.reshape((-1, a.shape[-1])) for part in parts for a in part]
    pair, twin = select(expert, base, blocks, width)

    place_of = {"o": x, "m": x - (1 - 2 * c), "p": x + (1 - 2 * c), "f": x + 2}

    def chip(at, dl):
        return (place_of[at] % 4) * 2 + (l + dl) % 2

    def offsets(chips):
        rows = [
            (chip(at, dl) * 2 + (c + half) % 2) * block for at, dl in chips for half in (0, 1)
        ]
        return jnp.stack(rows).astype(jnp.int32)

    def pieces(spread, chips):
        return [
            spread.found[at, dl, half, side] for at, dl in chips for half in (0, 1) for side in (0, 1)
        ]

    total = 16 * block

    def hidden_of(chips, token, *old):
        return ffn(offsets(chips), pieces(rows, chips), gate_panel, up_panel, total, token, old)

    token = jnp.zeros((8, 128), jnp.float32)
    rows = Spread()
    rows.open(pair, twin)
    hidden, token = hidden_of([("o", 0)], token)
    token = rows.first(token)
    rows.second()
    hidden, token = hidden_of([("o", 1), ("m", 0), ("p", 0)], token, hidden)
    token = rows.third(token)
    hidden, token = hidden_of([("m", 1), ("p", 1), ("f", 0)], token, hidden)
    token = rows.end(token)
    hidden, token = hidden_of([("f", 1)], token, hidden)

    def columns(keys):
        ids = [(chip(at, dl) * 2 + (c + half) % 2) * 2 + side for at, dl, half, side in keys]
        return jnp.stack(ids).astype(jnp.int32)

    def part(chips, token, old=None):
        keys = [
            (at, dl, half, side) for at, dl in chips for side in (0, 1) for half in (0, 1)
        ]
        found = [panels.found[key] for key in keys]
        return gram(columns(keys), scale, own, found, features, token, old)

    panels = Spread()
    panels.open(hidden)
    token = panels.first(token)
    panels.second()
    own = hidden
    out, token, own = part([("o", 0), ("o", 1), ("m", 0), ("p", 0)], token)
    token = panels.third(token)
    out, token = part([("m", 1), ("p", 1), ("f", 0)], token, out)
    token = panels.end(token)
    out, token = part([("f", 1)], token, out)
    return out[None]


def solution(mesh):
    fine = Mesh(mesh.devices.reshape(4, 2, 4, 2, 2), AXES)
    rows = P(AXES, None)
    weight = P(("y", "h"), None, ("x", "l", "c"))
    return jax.shard_map(
        local,
        mesh=fine,
        in_specs=(rows, rows, P(), weight, weight),
        out_specs=P(("y", "h"), ("x", "l", "c"), None),
        check_vma=False,
    )
```

```python
import functools

import jax
import jax.numpy as jnp
from jax import lax
from jax.experimental import pallas as pl
from jax.experimental.pallas import tpu as pltpu
from jax.sharding import Mesh
from jax.sharding import PartitionSpec as P

AXES = ("y", "h", "x", "l", "c")
ROUTE_LANES = 128
VMEM_BYTES = 56 * 1024 * 1024
SLOTS = 12
INTERPRET = False
ANY = pl.BlockSpec(memory_space=pl.ANY)
SMEM = pl.BlockSpec(memory_space=pltpu.SMEM)
VMEM = pl.BlockSpec(memory_space=pltpu.VMEM)


def ring_hop(a, axis):
    pairs = [(2 * i + c, 2 * ((i + (1, 3)[c]) % 4) + c) for i in range(4) for c in range(2)]
    return lax.ppermute(a, (axis, "c"), pairs)


def ring_back(a, axis):
    pairs = [(2 * i + c, 2 * ((i + (3, 1)[c]) % 4) + c) for i in range(4) for c in range(2)]
    return lax.ppermute(a, (axis, "c"), pairs)


def swap(a, axis):
    return lax.ppermute(a, axis, [(0, 1), (1, 0)])


def far_swap(a):
    return lax.ppermute(a, ("h", "l"), [(0, 3), (3, 0), (1, 2), (2, 1)])


def after(a, *others):
    return lax.optimization_barrier((a,) + others)[0]


def tie(a, token):
    return lax.optimization_barrier((a, token))


def cost(microseconds):
    return pl.CostEstimate(
        flops=int(microseconds * 1_150_000_000), bytes_accessed=1_000_000, transcendentals=0
    )


def select_kernel(n, width, expert_ref, base_ref, *rest):
    sources, (own_ref, twin_ref, held, sems) = rest[:n], rest[n:]
    copies, row = [], 0
    for i, source in enumerate(sources):
        rows = pl.ds(row, source.shape[0])
        copies.append(pltpu.make_async_copy(source, held.at[rows], sems.at[i]))
        copies[-1].start()
        row += source.shape[0]
    tokens, out_rows = held.shape[0], 2 * own_ref.shape[1]
    first = lax.broadcasted_iota(jnp.int32, (tokens, tokens), 0)
    second = lax.broadcasted_iota(jnp.int32, (tokens, tokens), 1)
    earlier = jnp.logical_and(first // 16 == second // 16, first < second)
    earlier = earlier.astype(jnp.float32).astype(jnp.bfloat16)
    lane = lax.broadcasted_iota(jnp.int32, (tokens, ROUTE_LANES), 1)
    places = lax.broadcasted_iota(jnp.int32, (out_rows, tokens), 0).astype(jnp.float32)
    ones = jnp.ones((16, ROUTE_LANES), jnp.bfloat16)
    for copy in copies:
        copy.wait()
    named = held[:, width:].astype(jnp.float32) == expert_ref[0].astype(jnp.float32)
    named = jnp.logical_and(named, lane < 2).astype(jnp.float32).astype(jnp.bfloat16)
    named = lax.dot_general(
        ones, named, (((1,), (1,)), ((), ())), preferred_element_type=jnp.float32
    )
    rank = jnp.dot(named.astype(jnp.bfloat16), earlier, preferred_element_type=jnp.float32)
    place = jnp.where(named[0:1, :] > 0.5, base_ref[0:1, :] + rank[0:1, :], -1.0)
    pick = (places == place).astype(jnp.float32).astype(jnp.bfloat16)
    half = width // 2
    for side, start in ((0, half), (1, 0)):
        got = jnp.dot(pick, held[:, start : start + half], preferred_element_type=jnp.float32)
        got = got.astype(jnp.bfloat16)
        own_ref[side] = got[: out_rows // 2]
        twin_ref[side] = got[out_rows // 2 :]


def select(expert, base, blocks, width):
    tokens = sum(b.shape[0] for b in blocks)
    half = jax.ShapeDtypeStruct((2, tokens // 32 * SLOTS, width // 2), jnp.bfloat16)
    return pl.pallas_call(
        functools.partial(select_kernel, len(blocks), width),
        out_shape=(half, half),
        in_specs=[SMEM, VMEM] + [ANY] * len(blocks),
        out_specs=(VMEM, VMEM),
        scratch_shapes=[
            pltpu.VMEM((tokens, blocks[0].shape[1]), jnp.bfloat16),
            pltpu.SemaphoreType.DMA((len(blocks),)),
        ],
        compiler_params=pltpu.CompilerParams(vmem_limit_bytes=VMEM_BYTES),
        cost_estimate=cost(3),
        interpret=INTERPRET,
    )(expert, base, *blocks)


def ffn_kernel(blocks, n_arrays, n_old, offsets_ref, *rest):
    arrays, (gate_hbm, up_hbm) = rest[:n_arrays], rest[n_arrays : n_arrays + 2]
    (
        out_ref,
        token_ref,
        rows,
        gate_held,
        up_held,
        result,
        sems,
        weight_sems,
        out_sems,
    ) = rest[n_arrays + 2 + n_old :]
    token_ref[...] = jnp.zeros_like(token_ref)
    piece_rows = rows.shape[0] // len(blocks)
    width, half = rows.shape[1] // 2, gate_held.shape[1] // 2
    copies = []
    for i, parts in enumerate(blocks):
        for array, start, count in parts:
            for side in range(2):
                target = rows.at[
                    pl.ds(i * piece_rows + start, count), pl.ds(side * width, width)
                ]
                copies.append(
                    pltpu.make_async_copy(
                        arrays[array].at[1 - side], target, sems.at[len(copies)]
                    )
                )
    weight_copies = []
    for q in range(2):
        cols = pl.ds(q * half, half)
        for j, (src, dst) in enumerate(((gate_hbm, gate_held), (up_hbm, up_held))):
            weight_copies.append(
                pltpu.make_async_copy(src.at[:, cols], dst.at[:, cols], weight_sems.at[2 * q + j])
            )
    for copy in weight_copies[:2] + copies + weight_copies[2:]:
        copy.start()
    for copy in copies:
        copy.wait()
    sent = []
    for q in range(2):
        weight_copies[2 * q].wait()
        weight_copies[2 * q + 1].wait()
        cols = slice(q * half, (q + 1) * half)
        gate = jnp.dot(rows[...], gate_held[:, cols], preferred_element_type=jnp.float32)
        up = jnp.dot(rows[...], up_held[:, cols], preferred_element_type=jnp.float32)
        result[q] = (gate / (1.0 + jnp.exp(-gate)) * up).astype(jnp.bfloat16)
        for i in range(len(blocks)):
            to = pl.ds(pl.multiple_of(offsets_ref[i], 16), piece_rows)
            sent.append(
                pltpu.make_async_copy(
                    result.at[q, pl.ds(i * piece_rows, piece_rows)],
                    out_ref.at[1 - q, to],
                    out_sems.at[q, i],
                )
            )
            sent[-1].start()
    for copy in sent:
        copy.wait()


def indexed(blocks):
    arrays, sources = [], []
    for parts in blocks:
        sources.append([])
        start = 0
        for array in parts:
            at = [i for i, known in enumerate(arrays) if known is array]
            if not at:
                arrays.append(array)
                at = [len(arrays) - 1]
            sources[-1].append((at[0], start, array.shape[1]))
            start += array.shape[1]
    return arrays, sources, start


def ffn(offsets, blocks, wg, wu, total_rows, token, old=()):
    arrays, sources, piece_rows = indexed(blocks)
    width, panel = wg.shape
    rows = len(blocks) * piece_rows
    out = jax.ShapeDtypeStruct((2, total_rows, panel // 2), jnp.bfloat16)
    first_old = 4 + len(arrays)
    return pl.pallas_call(
        functools.partial(ffn_kernel, sources, len(arrays), len(old) + 1),
        out_shape=(out, jax.ShapeDtypeStruct((8, 128), jnp.float32)),
        in_specs=[SMEM] + [ANY] * (len(arrays) + 3 + len(old)),
        out_specs=(ANY, VMEM),
        scratch_shapes=[
            pltpu.VMEM((rows, width), jnp.bfloat16),
            pltpu.VMEM(wg.shape, jnp.bfloat16),
            pltpu.VMEM(wu.shape, jnp.bfloat16),
            pltpu.VMEM((2, rows, panel // 2), jnp.bfloat16),
            pltpu.SemaphoreType.DMA((2 * sum(len(parts) for parts in sources),)),
            pltpu.SemaphoreType.DMA((4,)),
            pltpu.SemaphoreType.DMA((2, len(blocks))),
        ],
        input_output_aliases={first_old + i: i for i in range(len(old))},
        compiler_params=pltpu.CompilerParams(vmem_limit_bytes=VMEM_BYTES),
        cost_estimate=cost(1),
        interpret=INTERPRET,
    )(offsets, *arrays, wg, wu, token, *old)


def gram_kernel(sources, n_arrays, first, extra, ids_ref, scale_ref, *rest):
    own_ref, *arrays = rest[: 1 + n_arrays]
    out_ref, token_ref, *rest = rest[1 + n_arrays + extra :]
    if first:
        turned, own_held, held, result, own_sem, in_sems, out_sems = rest
    else:
        turned, held, result, own_sem, in_sems, out_sems = rest
    token_ref[...] = jnp.zeros_like(token_ref)
    half = held.shape[3]
    depth, count = held.shape[0], len(sources)

    def fetch(p):
        copies = []
        for k, (array, start, rows) in enumerate(sources[p]):
            target = held.at[p % depth, :, pl.ds(start, rows)]
            copies.append(pltpu.make_async_copy(arrays[array], target, in_sems.at[p % depth, k]))
            copies[-1].start()
        return copies

    own = pltpu.make_async_copy(own_ref, own_held if first else turned, own_sem)
    own.start()
    fetched = {0: fetch(0)}
    own.wait()
    if first:
        for side in range(2):
            turned[side * half : (side + 1) * half, :] = own_held[1 - side].T
    fetched.update({p: fetch(p) for p in range(1, min(depth, count))})
    sent = {}
    for p in range(count):
        for copy in fetched[p]:
            copy.wait()
        if p >= 2:
            sent[p - 2].wait()
        for side in range(2):
            total = jnp.dot(
                turned[...], held[p % depth, 1 - side], preferred_element_type=jnp.float32
            )
            result[p % 2, :, side * half : (side + 1) * half] = total * scale_ref[0]
        if p + depth < count:
            fetched[p + depth] = fetch(p + depth)
        cols = pl.ds(pl.multiple_of(ids_ref[p] * 2 * half, 2 * half), 2 * half)
        sent[p] = pltpu.make_async_copy(result.at[p % 2], out_ref.at[:, cols], out_sems.at[p % 2])
        sent[p].start()
    for p in range(max(0, count - 2), count):
        sent[p].wait()


def gram(ids, scale, own, pairs, features, token, old=None):
    arrays, sources, rows = indexed(pairs)
    half = arrays[0].shape[2]
    first = own.ndim == 3
    extra = 1 if old is None else 2
    turned = ((2 * half, rows), jnp.bfloat16)
    return pl.pallas_call(
        functools.partial(gram_kernel, sources, len(arrays), first, extra),
        out_shape=(
            jax.ShapeDtypeStruct((2 * half, features), jnp.float32),
            jax.ShapeDtypeStruct((8, 128), jnp.float32),
        )
        + ((jax.ShapeDtypeStruct(*turned),) if first else ()),
        in_specs=[SMEM] * 2 + [ANY] * (1 + len(arrays) + extra),
        out_specs=(ANY, VMEM) + ((VMEM,) if first else ()),
        scratch_shapes=[
            pltpu.VMEM((2, rows, half), jnp.bfloat16) if first else pltpu.VMEM(*turned),
            pltpu.VMEM((3, 2, rows, half), jnp.bfloat16),
            pltpu.VMEM((2, 2 * half, 2 * half), jnp.float32),
            pltpu.SemaphoreType.DMA(()),
            pltpu.SemaphoreType.DMA((3, 2)),
            pltpu.SemaphoreType.DMA((2,)),
        ],
        input_output_aliases={} if old is None else {4 + len(arrays): 0},
        compiler_params=pltpu.CompilerParams(vmem_limit_bytes=VMEM_BYTES),
        cost_estimate=cost(1),
        interpret=INTERPRET,
    )(ids, scale, own, *arrays, token, *([] if old is None else [old]))


class Spread:
    def __init__(self):
        self.found = {}

    def keep(self, arrays, at, dl, core):
        twins = [swap(array, "c") for array in arrays]
        at_twin = {"o": "o", "m": "p", "f": "f"}[at]
        self.found[at, dl, core] = arrays
        self.found[at_twin, dl, 1 - core] = twins
        return twins

    def open(self, pair, twin=None):
        beside, near = swap(pair, "l"), ring_hop(pair, "x")
        if twin is None:
            twin = swap(pair, "c")
        near_twin = ring_hop(twin, "x")
        self.found["o", 0, 0], self.found["o", 0, 1] = [pair], [twin]
        self.moved = (beside, near, near_twin)

    def first(self, token):
        beside, near, near_twin = self.moved
        beside, near, token = lax.optimization_barrier((beside, near, token))
        self.moved = (beside, near, near_twin)
        return token

    def second(self):
        beside, near, near_twin = self.moved
        near_beside = swap(near, "l")
        far = ring_hop(near, "x")
        (twin,) = self.keep([beside], "o", 1, 0)
        beside_near = ring_hop(twin, "x")
        self.keep([near], "m", 0, 0)
        self.keep([near_twin], "m", 0, 1)
        self.moved = (far, near_beside, beside_near)

    def third(self, token):
        far, near_beside, beside_near = self.moved
        far, token = tie(far, token)
        rows = far.shape[1] // 3
        over_l = swap(far[:, :rows], "l")
        near_beside, token = tie(near_beside, token)
        over_x = ring_hop(near_beside[:, rows:], "x")
        self.keep([near_beside], "m", 1, 0)
        beside_near, token = tie(beside_near, token)
        self.keep([beside_near], "m", 1, 1)
        self.keep([far], "f", 0, 0)
        self.moved = (over_l, over_x)
        return token

    def end(self, token):
        *moved, token = lax.optimization_barrier((*self.moved, token))
        self.keep(moved, "f", 1, 0)
        return token


def local(tokens, routes, counts, gate_weight, up_weight):
    x, l, c = lax.axis_index("x"), lax.axis_index("l"), lax.axis_index("c")
    expert = lax.axis_index("y") * 2 + lax.axis_index("h")
    gate_panel, up_panel = gate_weight[0], up_weight[0]
    width, panel = gate_panel.shape
    features = 16 * panel
    routed_total = jnp.sum(jnp.where(jnp.arange(8) == expert, counts, 0)).astype(jnp.float32)
    scale = (2.0 / routed_total).reshape(1)
    expert = expert.reshape(1).astype(jnp.int32)

    tagged = jnp.concatenate(
        [tokens, jnp.pad(routes.astype(tokens.dtype), ((0, 0), (0, ROUTE_LANES - 2)))], axis=1
    )
    pair = jnp.stack([tagged, far_swap(tagged)])
    near, back = ring_hop(pair, "y"), ring_back(pair, "y")
    far = lax.ppermute(pair, "y", [(i, (i + 2) % 4) for i in range(4)])
    parts = [(a, swap(a, "c")) for a in (pair, near, back, far)]

    block = 8 * SLOTS
    y_near, y_back = 1 + c, 2 - c
    base = []
    for y_mine, y_twin in ((0, 0), (y_near, y_back), (y_back, y_near), (3, 3)):
        for dc, y_of in ((0, y_mine), (1, y_twin)):
            base += [dc * block + (2 * y_of + dh) * SLOTS for dh in (0, 1)]
    base = jnp.stack([jnp.asarray(b, jnp.int32) for b in base])
    base = jnp.broadcast_to(jnp.repeat(base, 16).astype(jnp.float32), (8, 256))
    blocks = [a.reshape((-1, a.shape[-1])) for part in parts for a in part]
    pair, twin = select(expert, base, blocks, width)

    place_of = {"o": x, "m": x - (1 - 2 * c), "p": x + (1 - 2 * c), "f": x + 2}

    def chip(at, dl):
        return (place_of[at] % 4) * 2 + (l + dl) % 2

    def offsets(chips):
        rows = [
            (chip(at, dl) * 2 + (c + half) % 2) * block for at, dl in chips for half in (0, 1)
        ]
        return jnp.stack(rows).astype(jnp.int32)

    def blocks_of(spread, chips):
        return [spread.found[at, dl, core] for at, dl in chips for core in (0, 1)]

    total = 16 * block

    def hidden_of(chips, token, *old):
        return ffn(
            offsets(chips), blocks_of(rows, chips), gate_panel, up_panel, total, token, old
        )

    token = jnp.zeros((8, 128), jnp.float32)
    rows = Spread()
    rows.open(pair, twin)
    hidden, token = hidden_of([("o", 0)], token)
    token = rows.first(token)
    rows.second()
    hidden, token = hidden_of([("o", 1), ("m", 0), ("p", 0)], token, hidden)
    token = rows.third(token)
    hidden, token = hidden_of([("m", 1), ("p", 1), ("f", 0)], token, hidden)
    token = rows.end(token)
    hidden, token = hidden_of([("f", 1)], token, hidden)

    def part(chips, token, old=None):
        ids = [chip(at, dl) * 2 + (c + core) % 2 for at, dl in chips for core in (0, 1)]
        ids = jnp.stack(ids).astype(jnp.int32)
        return gram(ids, scale, own, blocks_of(panels, chips), features, token, old)

    panels = Spread()
    panels.open(hidden)
    token = panels.first(token)
    panels.second()
    own = hidden
    out, token, own = part([("o", 0), ("o", 1), ("m", 0), ("p", 0)], token)
    token = panels.third(token)
    out, token = part([("m", 1), ("p", 1), ("f", 0)], token, out)
    token = panels.end(token)
    out, token = part([("f", 1)], token, out)
    return out[None]


def solution(mesh):
    fine = Mesh(mesh.devices.reshape(4, 2, 4, 2, 2), AXES)
    rows = P(AXES, None)
    weight = P(("y", "h"), None, ("x", "l", "c"))
    return jax.shard_map(
        local,
        mesh=fine,
        in_specs=(rows, rows, P(), weight, weight),
        out_specs=P(("y", "h"), ("x", "l", "c"), None),
        check_vma=False,
    )
```

```python
import functools

import jax
import jax.numpy as jnp
from jax import lax
from jax.experimental import pallas as pl
from jax.experimental.pallas import tpu as pltpu
from jax.sharding import Mesh
from jax.sharding import PartitionSpec as P

AXES = ("y", "h", "x", "l", "c")
ROUTE_LANES = 128
VMEM_BYTES = 56 * 1024 * 1024
SLOTS = 12
INTERPRET = False
ANY = pl.BlockSpec(memory_space=pl.ANY)
SMEM = pl.BlockSpec(memory_space=pltpu.SMEM)
VMEM = pl.BlockSpec(memory_space=pltpu.VMEM)


def ring_hop(a, axis):
    pairs = [(2 * i + c, 2 * ((i + (1, 3)[c]) % 4) + c) for i in range(4) for c in range(2)]
    return lax.ppermute(a, (axis, "c"), pairs)


def ring_back(a, axis):
    pairs = [(2 * i + c, 2 * ((i + (3, 1)[c]) % 4) + c) for i in range(4) for c in range(2)]
    return lax.ppermute(a, (axis, "c"), pairs)


def swap(a, axis):
    return lax.ppermute(a, axis, [(0, 1), (1, 0)])


def far_swap(a):
    return lax.ppermute(a, ("h", "l"), [(0, 3), (3, 0), (1, 2), (2, 1)])


def after(a, *others):
    return lax.optimization_barrier((a,) + others)[0]


def tie(a, token):
    return lax.optimization_barrier((a, token))


def cost(microseconds):
    return pl.CostEstimate(
        flops=int(microseconds * 1_150_000_000), bytes_accessed=1_000_000, transcendentals=0
    )


def select_kernel(n, width, expert_ref, base_ref, *rest):
    sources, (own_ref, twin_ref, held, sems) = rest[:n], rest[n:]
    copies, row = [], 0
    for i, source in enumerate(sources):
        rows = pl.ds(row, source.shape[0])
        copies.append(pltpu.make_async_copy(source, held.at[rows], sems.at[i]))
        copies[-1].start()
        row += source.shape[0]
    tokens, out_rows = held.shape[0], 2 * own_ref.shape[1]
    first = lax.broadcasted_iota(jnp.int32, (tokens, tokens), 0)
    second = lax.broadcasted_iota(jnp.int32, (tokens, tokens), 1)
    earlier = jnp.logical_and(first // 16 == second // 16, first < second)
    earlier = earlier.astype(jnp.float32).astype(jnp.bfloat16)
    lane = lax.broadcasted_iota(jnp.int32, (tokens, ROUTE_LANES), 1)
    places = lax.broadcasted_iota(jnp.int32, (out_rows, tokens), 0).astype(jnp.float32)
    ones = jnp.ones((16, ROUTE_LANES), jnp.bfloat16)
    for copy in copies:
        copy.wait()
    named = held[:, width:].astype(jnp.float32) == expert_ref[0].astype(jnp.float32)
    named = jnp.logical_and(named, lane < 2).astype(jnp.float32).astype(jnp.bfloat16)
    named = lax.dot_general(
        ones, named, (((1,), (1,)), ((), ())), preferred_element_type=jnp.float32
    )
    rank = jnp.dot(named.astype(jnp.bfloat16), earlier, preferred_element_type=jnp.float32)
    place = jnp.where(named[0:1, :] > 0.5, base_ref[0:1, :] + rank[0:1, :], -1.0)
    pick = (places == place).astype(jnp.float32).astype(jnp.bfloat16)
    half = width // 2
    for side, start in ((0, half), (1, 0)):
        got = jnp.dot(pick, held[:, start : start + half], preferred_element_type=jnp.float32)
        got = got.astype(jnp.bfloat16)
        own_ref[side] = got[: out_rows // 2]
        twin_ref[side] = got[out_rows // 2 :]


def select(expert, base, blocks, width):
    tokens = sum(b.shape[0] for b in blocks)
    half = jax.ShapeDtypeStruct((2, tokens // 32 * SLOTS, width // 2), jnp.bfloat16)
    return pl.pallas_call(
        functools.partial(select_kernel, len(blocks), width),
        out_shape=(half, half),
        in_specs=[SMEM, VMEM] + [ANY] * len(blocks),
        out_specs=(VMEM, VMEM),
        scratch_shapes=[
            pltpu.VMEM((tokens, blocks[0].shape[1]), jnp.bfloat16),
            pltpu.SemaphoreType.DMA((len(blocks),)),
        ],
        compiler_params=pltpu.CompilerParams(vmem_limit_bytes=VMEM_BYTES),
        cost_estimate=cost(3),
        interpret=INTERPRET,
    )(expert, base, *blocks)


def ffn_kernel(blocks, n_arrays, n_old, offsets_ref, *rest):
    arrays, (gate_hbm, up_hbm) = rest[:n_arrays], rest[n_arrays : n_arrays + 2]
    (
        out_ref,
        token_ref,
        rows,
        gate_held,
        up_held,
        result,
        sems,
        weight_sems,
        out_sems,
    ) = rest[n_arrays + 2 + n_old :]
    token_ref[...] = jnp.zeros_like(token_ref)
    piece_rows = rows.shape[0] // len(blocks)
    width, half = rows.shape[1] // 2, gate_held.shape[1] // 2
    copies = []
    for i, parts in enumerate(blocks):
        for array, start, count in parts:
            for side in range(2):
                target = rows.at[
                    pl.ds(i * piece_rows + start, count), pl.ds(side * width, width)
                ]
                copies.append(
                    pltpu.make_async_copy(
                        arrays[array].at[1 - side], target, sems.at[len(copies)]
                    )
                )
    weight_copies = []
    for q in range(2):
        cols = pl.ds(q * half, half)
        for j, (src, dst) in enumerate(((gate_hbm, gate_held), (up_hbm, up_held))):
            weight_copies.append(
                pltpu.make_async_copy(src.at[:, cols], dst.at[:, cols], weight_sems.at[2 * q + j])
            )
    late = weight_copies[2:] if len(blocks) > 2 else []
    for copy in weight_copies[:2] + copies + ([] if late else weight_copies[2:]):
        copy.start()
    for copy in copies:
        copy.wait()
    sent = []
    for q in range(2):
        weight_copies[2 * q].wait()
        weight_copies[2 * q + 1].wait()
        if q == 0:
            for copy in late:
                copy.start()
        cols = slice(q * half, (q + 1) * half)
        gate = jnp.dot(rows[...], gate_held[:, cols], preferred_element_type=jnp.float32)
        up = jnp.dot(rows[...], up_held[:, cols], preferred_element_type=jnp.float32)
        result[q] = (gate / (1.0 + jnp.exp(-gate)) * up).astype(jnp.bfloat16)
        for i in range(len(blocks)):
            to = pl.ds(pl.multiple_of(offsets_ref[i], 16), piece_rows)
            sent.append(
                pltpu.make_async_copy(
                    result.at[q, pl.ds(i * piece_rows, piece_rows)],
                    out_ref.at[1 - q, to],
                    out_sems.at[q, i],
                )
            )
            sent[-1].start()
    for copy in sent:
        copy.wait()


def indexed(blocks):
    arrays, sources = [], []
    for parts in blocks:
        sources.append([])
        start = 0
        for array in parts:
            at = [i for i, known in enumerate(arrays) if known is array]
            if not at:
                arrays.append(array)
                at = [len(arrays) - 1]
            sources[-1].append((at[0], start, array.shape[1]))
            start += array.shape[1]
    return arrays, sources, start


def ffn(offsets, blocks, wg, wu, total_rows, token, old=()):
    arrays, sources, piece_rows = indexed(blocks)
    width, panel = wg.shape
    rows = len(blocks) * piece_rows
    out = jax.ShapeDtypeStruct((2, total_rows, panel // 2), jnp.bfloat16)
    first_old = 4 + len(arrays)
    return pl.pallas_call(
        functools.partial(ffn_kernel, sources, len(arrays), len(old) + 1),
        out_shape=(out, jax.ShapeDtypeStruct((8, 128), jnp.float32)),
        in_specs=[SMEM] + [ANY] * (len(arrays) + 3 + len(old)),
        out_specs=(ANY, VMEM),
        scratch_shapes=[
            pltpu.VMEM((rows, width), jnp.bfloat16),
            pltpu.VMEM(wg.shape, jnp.bfloat16),
            pltpu.VMEM(wu.shape, jnp.bfloat16),
            pltpu.VMEM((2, rows, panel // 2), jnp.bfloat16),
            pltpu.SemaphoreType.DMA((2 * sum(len(parts) for parts in sources),)),
            pltpu.SemaphoreType.DMA((4,)),
            pltpu.SemaphoreType.DMA((2, len(blocks))),
        ],
        input_output_aliases={first_old + i: i for i in range(len(old))},
        compiler_params=pltpu.CompilerParams(vmem_limit_bytes=VMEM_BYTES),
        cost_estimate=cost(1),
        interpret=INTERPRET,
    )(offsets, *arrays, wg, wu, token, *old)


def gram_kernel(sources, n_arrays, first, extra, ids_ref, scale_ref, *rest):
    own_ref, *arrays = rest[: 1 + n_arrays]
    out_ref, token_ref, *rest = rest[1 + n_arrays + extra :]
    if first:
        turned, own_held, held, result, own_sem, in_sems, out_sems = rest
    else:
        turned, held, result, own_sem, in_sems, out_sems = rest
    token_ref[...] = jnp.zeros_like(token_ref)
    half = held.shape[3]
    depth, count = held.shape[0], len(sources)

    def fetch(p):
        copies = []
        for k, (array, start, rows) in enumerate(sources[p]):
            target = held.at[p % depth, :, pl.ds(start, rows)]
            copies.append(pltpu.make_async_copy(arrays[array], target, in_sems.at[p % depth, k]))
            copies[-1].start()
        return copies

    own = pltpu.make_async_copy(own_ref, own_held if first else turned, own_sem)
    own.start()
    fetched = {0: fetch(0)}
    own.wait()
    if first:
        for side in range(2):
            turned[side * half : (side + 1) * half, :] = own_held[1 - side].T
    fetched.update({p: fetch(p) for p in range(1, min(depth, count))})
    sent = {}
    for p in range(count):
        for copy in fetched[p]:
            copy.wait()
        if p >= 2:
            sent[p - 2].wait()
        for side in range(2):
            total = jnp.dot(
                turned[...], held[p % depth, 1 - side], preferred_element_type=jnp.float32
            )
            result[p % 2, :, side * half : (side + 1) * half] = total * scale_ref[0]
        if p + depth < count:
            fetched[p + depth] = fetch(p + depth)
        cols = pl.ds(pl.multiple_of(ids_ref[p] * 2 * half, 2 * half), 2 * half)
        sent[p] = pltpu.make_async_copy(result.at[p % 2], out_ref.at[:, cols], out_sems.at[p % 2])
        sent[p].start()
    for p in range(max(0, count - 2), count):
        sent[p].wait()


def gram(ids, scale, own, pairs, features, token, old=None):
    arrays, sources, rows = indexed(pairs)
    half = arrays[0].shape[2]
    first = own.ndim == 3
    extra = 1 if old is None else 2
    turned = ((2 * half, rows), jnp.bfloat16)
    return pl.pallas_call(
        functools.partial(gram_kernel, sources, len(arrays), first, extra),
        out_shape=(
            jax.ShapeDtypeStruct((2 * half, features), jnp.float32),
            jax.ShapeDtypeStruct((8, 128), jnp.float32),
        )
        + ((jax.ShapeDtypeStruct(*turned),) if first else ()),
        in_specs=[SMEM] * 2 + [ANY] * (1 + len(arrays) + extra),
        out_specs=(ANY, VMEM) + ((VMEM,) if first else ()),
        scratch_shapes=[
            pltpu.VMEM((2, rows, half), jnp.bfloat16) if first else pltpu.VMEM(*turned),
            pltpu.VMEM((3, 2, rows, half), jnp.bfloat16),
            pltpu.VMEM((2, 2 * half, 2 * half), jnp.float32),
            pltpu.SemaphoreType.DMA(()),
            pltpu.SemaphoreType.DMA((3, 2)),
            pltpu.SemaphoreType.DMA((2,)),
        ],
        input_output_aliases={} if old is None else {4 + len(arrays): 0},
        compiler_params=pltpu.CompilerParams(vmem_limit_bytes=VMEM_BYTES),
        cost_estimate=cost(1),
        interpret=INTERPRET,
    )(ids, scale, own, *arrays, token, *([] if old is None else [old]))


class Spread:
    def __init__(self):
        self.found = {}

    def keep(self, arrays, at, dl, core):
        twins = [swap(array, "c") for array in arrays]
        at_twin = {"o": "o", "m": "p", "f": "f"}[at]
        self.found[at, dl, core] = arrays
        self.found[at_twin, dl, 1 - core] = twins
        return twins

    def open(self, pair, twin=None):
        beside, near = swap(pair, "l"), ring_hop(pair, "x")
        if twin is None:
            twin = swap(pair, "c")
        near_twin = ring_hop(twin, "x")
        self.found["o", 0, 0], self.found["o", 0, 1] = [pair], [twin]
        self.moved = (beside, near, near_twin)

    def first(self, token):
        beside, near, near_twin = self.moved
        near, token = tie(near, token)
        near_beside, far = swap(near, "l"), ring_hop(near, "x")
        beside, near_twin, token = lax.optimization_barrier((beside, near_twin, token))
        (twin,) = self.keep([beside], "o", 1, 0)
        beside_near = ring_hop(twin, "x")
        self.keep([near], "m", 0, 0)
        self.keep([near_twin], "m", 0, 1)
        self.moved = (far, near_beside, beside_near)
        return token

    def third(self, token):
        far, near_beside, beside_near = self.moved
        far, token = tie(far, token)
        rows = far.shape[1] // 3
        over_l = swap(far[:, :rows], "l")
        near_beside, token = tie(near_beside, token)
        over_x = ring_hop(near_beside[:, rows:], "x")
        self.keep([near_beside], "m", 1, 0)
        beside_near, token = tie(beside_near, token)
        self.keep([beside_near], "m", 1, 1)
        self.keep([far], "f", 0, 0)
        self.moved = (over_l, over_x)
        return token

    def end(self, token):
        *moved, token = lax.optimization_barrier((*self.moved, token))
        self.keep(moved, "f", 1, 0)
        return token


def local(tokens, routes, counts, gate_weight, up_weight):
    x, l, c = lax.axis_index("x"), lax.axis_index("l"), lax.axis_index("c")
    expert = lax.axis_index("y") * 2 + lax.axis_index("h")
    gate_panel, up_panel = gate_weight[0], up_weight[0]
    width, panel = gate_panel.shape
    features = 16 * panel
    routed_total = jnp.sum(jnp.where(jnp.arange(8) == expert, counts, 0)).astype(jnp.float32)
    scale = (2.0 / routed_total).reshape(1)
    expert = expert.reshape(1).astype(jnp.int32)

    tagged = jnp.concatenate(
        [tokens, jnp.pad(routes.astype(tokens.dtype), ((0, 0), (0, ROUTE_LANES - 2)))], axis=1
    )
    pair = jnp.stack([tagged, far_swap(tagged)])
    near, back = ring_hop(pair, "y"), ring_back(pair, "y")
    far = lax.ppermute(pair, "y", [(i, (i + 2) % 4) for i in range(4)])
    parts = [(a, swap(a, "c")) for a in (pair, near, back, far)]

    block = 8 * SLOTS
    y_near, y_back = 1 + c, 2 - c
    base = []
    for y_mine, y_twin in ((0, 0), (y_near, y_back), (y_back, y_near), (3, 3)):
        for dc, y_of in ((0, y_mine), (1, y_twin)):
            base += [dc * block + (2 * y_of + dh) * SLOTS for dh in (0, 1)]
    base = jnp.stack([jnp.asarray(b, jnp.int32) for b in base])
    base = jnp.broadcast_to(jnp.repeat(base, 16).astype(jnp.float32), (8, 256))
    blocks = [a.reshape((-1, a.shape[-1])) for part in parts for a in part]
    pair, twin = select(expert, base, blocks, width)

    place_of = {"o": x, "m": x - (1 - 2 * c), "p": x + (1 - 2 * c), "f": x + 2}

    def chip(at, dl):
        return (place_of[at] % 4) * 2 + (l + dl) % 2

    def offsets(chips):
        rows = [
            (chip(at, dl) * 2 + (c + half) % 2) * block for at, dl in chips for half in (0, 1)
        ]
        return jnp.stack(rows).astype(jnp.int32)

    def blocks_of(spread, chips):
        return [spread.found[at, dl, core] for at, dl in chips for core in (0, 1)]

    total = 16 * block

    def hidden_of(chips, token, *old):
        return ffn(
            offsets(chips), blocks_of(rows, chips), gate_panel, up_panel, total, token, old
        )

    token = jnp.zeros((8, 128), jnp.float32)
    rows = Spread()
    rows.open(pair, twin)
    hidden, token = hidden_of([("o", 0)], token)
    token = rows.first(token)
    hidden, token = hidden_of([("o", 1), ("m", 0), ("p", 0)], token, hidden)
    token = rows.third(token)
    hidden, token = hidden_of([("m", 1), ("p", 1), ("f", 0)], token, hidden)
    token = rows.end(token)
    hidden, token = hidden_of([("f", 1)], token, hidden)

    def part(chips, token, old=None):
        ids = [chip(at, dl) * 2 + (c + core) % 2 for at, dl in chips for core in (0, 1)]
        ids = jnp.stack(ids).astype(jnp.int32)
        return gram(ids, scale, own, blocks_of(panels, chips), features, token, old)

    panels = Spread()
    panels.open(hidden)
    token = panels.first(token)
    own = hidden
    out, token, own = part([("o", 0), ("o", 1), ("m", 0), ("p", 0)], token)
    token = panels.third(token)
    out, token = part([("m", 1), ("p", 1), ("f", 0)], token, out)
    token = panels.end(token)
    out, token = part([("f", 1)], token, out)
    return out[None]


def solution(mesh):
    fine = Mesh(mesh.devices.reshape(4, 2, 4, 2, 2), AXES)
    rows = P(AXES, None)
    weight = P(("y", "h"), None, ("x", "l", "c"))
    return jax.shard_map(
        local,
        mesh=fine,
        in_specs=(rows, rows, P(), weight, weight),
        out_specs=P(("y", "h"), ("x", "l", "c"), None),
        check_vma=False,
    )
```

```python
import functools

import jax
import jax.numpy as jnp
from jax import lax
from jax.experimental import pallas as pl
from jax.experimental.pallas import tpu as pltpu
from jax.sharding import Mesh
from jax.sharding import PartitionSpec as P

AXES = ("y", "h", "x", "l", "c")
ROUTE_LANES = 128
VMEM_BYTES = 56 * 1024 * 1024
SLOTS = 12
INTERPRET = False
ANY = pl.BlockSpec(memory_space=pl.ANY)
SMEM = pl.BlockSpec(memory_space=pltpu.SMEM)
VMEM = pl.BlockSpec(memory_space=pltpu.VMEM)


def ring_hop(a, axis):
    pairs = [(2 * i + c, 2 * ((i + (1, 3)[c]) % 4) + c) for i in range(4) for c in range(2)]
    return lax.ppermute(a, (axis, "c"), pairs)


def ring_back(a, axis):
    pairs = [(2 * i + c, 2 * ((i + (3, 1)[c]) % 4) + c) for i in range(4) for c in range(2)]
    return lax.ppermute(a, (axis, "c"), pairs)


def swap(a, axis):
    return lax.ppermute(a, axis, [(0, 1), (1, 0)])


def far_swap(a):
    return lax.ppermute(a, ("h", "l"), [(0, 3), (3, 0), (1, 2), (2, 1)])


def after(a, *others):
    return lax.optimization_barrier((a,) + others)[0]


def tie(a, token):
    return lax.optimization_barrier((a, token))


def cost(microseconds):
    return pl.CostEstimate(
        flops=int(microseconds * 1_150_000_000), bytes_accessed=1_000_000, transcendentals=0
    )


def select_kernel(n, width, expert_ref, base_ref, *rest):
    sources, (own_ref, twin_ref, held, sems) = rest[:n], rest[n:]
    copies, row = [], 0
    for i, source in enumerate(sources):
        rows = pl.ds(row, source.shape[0])
        copies.append(pltpu.make_async_copy(source, held.at[rows], sems.at[i]))
        copies[-1].start()
        row += source.shape[0]
    tokens, out_rows = held.shape[0], 2 * own_ref.shape[1]
    first = lax.broadcasted_iota(jnp.int32, (tokens, tokens), 0)
    second = lax.broadcasted_iota(jnp.int32, (tokens, tokens), 1)
    earlier = jnp.logical_and(first // 16 == second // 16, first < second)
    earlier = earlier.astype(jnp.float32).astype(jnp.bfloat16)
    lane = lax.broadcasted_iota(jnp.int32, (tokens, ROUTE_LANES), 1)
    places = lax.broadcasted_iota(jnp.int32, (out_rows, tokens), 0).astype(jnp.float32)
    ones = jnp.ones((16, ROUTE_LANES), jnp.bfloat16)
    for copy in copies:
        copy.wait()
    named = held[:, width:].astype(jnp.float32) == expert_ref[0].astype(jnp.float32)
    named = jnp.logical_and(named, lane < 2).astype(jnp.float32).astype(jnp.bfloat16)
    named = lax.dot_general(
        ones, named, (((1,), (1,)), ((), ())), preferred_element_type=jnp.float32
    )
    rank = jnp.dot(named.astype(jnp.bfloat16), earlier, preferred_element_type=jnp.float32)
    place = jnp.where(named[0:1, :] > 0.5, base_ref[0:1, :] + rank[0:1, :], -1.0)
    pick = (places == place).astype(jnp.float32).astype(jnp.bfloat16)
    half = width // 2
    for side, start in ((0, half), (1, 0)):
        got = jnp.dot(pick, held[:, start : start + half], preferred_element_type=jnp.float32)
        got = got.astype(jnp.bfloat16)
        own_ref[side] = got[: out_rows // 2]
        twin_ref[side] = got[out_rows // 2 :]


def select(expert, base, blocks, width):
    tokens = sum(b.shape[0] for b in blocks)
    half = jax.ShapeDtypeStruct((2, tokens // 32 * SLOTS, width // 2), jnp.bfloat16)
    return pl.pallas_call(
        functools.partial(select_kernel, len(blocks), width),
        out_shape=(half, half),
        in_specs=[SMEM, VMEM] + [ANY] * len(blocks),
        out_specs=(VMEM, VMEM),
        scratch_shapes=[
            pltpu.VMEM((tokens, blocks[0].shape[1]), jnp.bfloat16),
            pltpu.SemaphoreType.DMA((len(blocks),)),
        ],
        compiler_params=pltpu.CompilerParams(vmem_limit_bytes=VMEM_BYTES),
        cost_estimate=cost(3),
        interpret=INTERPRET,
    )(expert, base, *blocks)


def ffn_kernel(blocks, first, n_arrays, n_old, offsets_ref, *rest):
    arrays, (gate_hbm, up_hbm) = rest[:n_arrays], rest[n_arrays : n_arrays + 2]
    (
        out_ref,
        token_ref,
        rows,
        gate_held,
        up_held,
        result,
        sems,
        weight_sems,
        out_sems,
    ) = rest[n_arrays + 2 + n_old :]
    token_ref[...] = jnp.zeros_like(token_ref)
    piece_rows = rows.shape[0] // len(blocks)
    width, half = rows.shape[1] // 2, gate_held.shape[1] // 2
    copies = []
    for i, parts in enumerate(blocks):
        for array, start, count in parts:
            for side in range(2):
                target = rows.at[
                    pl.ds(i * piece_rows + start, count), pl.ds(side * width, width)
                ]
                copies.append(
                    pltpu.make_async_copy(
                        arrays[array].at[1 - side], target, sems.at[len(copies)]
                    )
                )
    weight_copies = []
    for q in range(2):
        cols = pl.ds(q * half, half)
        for j, (src, dst) in enumerate(((gate_hbm, gate_held), (up_hbm, up_held))):
            weight_copies.append(
                pltpu.make_async_copy(src.at[:, cols], dst.at[:, cols], weight_sems.at[2 * q + j])
            )
    late = weight_copies[2:] if len(blocks) > 2 else []
    for copy in weight_copies[:2] + copies + ([] if late else weight_copies[2:]):
        copy.start()
    for copy in copies:
        copy.wait()
    sent = []
    for q in range(2):
        weight_copies[2 * q].wait()
        weight_copies[2 * q + 1].wait()
        if q == 0:
            for copy in late:
                copy.start()
        cols = slice(q * half, (q + 1) * half)
        gate = jnp.dot(rows[...], gate_held[:, cols], preferred_element_type=jnp.float32)
        up = jnp.dot(rows[...], up_held[:, cols], preferred_element_type=jnp.float32)
        result[q] = (gate / (1.0 + jnp.exp(-gate)) * up).astype(jnp.bfloat16)
        for i in range(len(blocks)):
            to = pl.ds(pl.multiple_of(offsets_ref[first + i], 16), piece_rows)
            sent.append(
                pltpu.make_async_copy(
                    result.at[q, pl.ds(i * piece_rows, piece_rows)],
                    out_ref.at[1 - q, to],
                    out_sems.at[q, i],
                )
            )
            sent[-1].start()
    for copy in sent:
        copy.wait()


def indexed(blocks):
    arrays, sources = [], []
    for parts in blocks:
        sources.append([])
        start = 0
        for array in parts:
            at = [i for i, known in enumerate(arrays) if known is array]
            if not at:
                arrays.append(array)
                at = [len(arrays) - 1]
            sources[-1].append((at[0], start, array.shape[1]))
            start += array.shape[1]
    return arrays, sources, start


def ffn(offsets, first, blocks, wg, wu, total_rows, token, old=()):
    arrays, sources, piece_rows = indexed(blocks)
    width, panel = wg.shape
    rows = len(blocks) * piece_rows
    out = jax.ShapeDtypeStruct((2, total_rows, panel // 2), jnp.bfloat16)
    first_old = 4 + len(arrays)
    return pl.pallas_call(
        functools.partial(ffn_kernel, sources, first, len(arrays), len(old) + 1),
        out_shape=(out, jax.ShapeDtypeStruct((8, 128), jnp.float32)),
        in_specs=[SMEM] + [ANY] * (len(arrays) + 3 + len(old)),
        out_specs=(ANY, VMEM),
        scratch_shapes=[
            pltpu.VMEM((rows, width), jnp.bfloat16),
            pltpu.VMEM(wg.shape, jnp.bfloat16),
            pltpu.VMEM(wu.shape, jnp.bfloat16),
            pltpu.VMEM((2, rows, panel // 2), jnp.bfloat16),
            pltpu.SemaphoreType.DMA((2 * sum(len(parts) for parts in sources),)),
            pltpu.SemaphoreType.DMA((4,)),
            pltpu.SemaphoreType.DMA((2, len(blocks))),
        ],
        input_output_aliases={first_old + i: i for i in range(len(old))},
        compiler_params=pltpu.CompilerParams(vmem_limit_bytes=VMEM_BYTES),
        cost_estimate=cost(1),
        interpret=INTERPRET,
    )(offsets, *arrays, wg, wu, token, *old)


def gram_kernel(sources, start, n_arrays, first, extra, ids_ref, scale_ref, *rest):
    own_ref, *arrays = rest[: 1 + n_arrays]
    out_ref, token_ref, *rest = rest[1 + n_arrays + extra :]
    if first:
        turned, own_held, held, result, own_sem, in_sems, out_sems = rest
    else:
        turned, held, result, own_sem, in_sems, out_sems = rest
    token_ref[...] = jnp.zeros_like(token_ref)
    half = held.shape[3]
    depth, count = held.shape[0], len(sources)

    def fetch(p):
        copies = []
        for k, (array, row, rows) in enumerate(sources[p]):
            target = held.at[p % depth, :, pl.ds(row, rows)]
            copies.append(pltpu.make_async_copy(arrays[array], target, in_sems.at[p % depth, k]))
            copies[-1].start()
        return copies

    own = pltpu.make_async_copy(own_ref, own_held if first else turned, own_sem)
    own.start()
    fetched = {0: fetch(0)}
    own.wait()
    if first:
        for side in range(2):
            turned[side * half : (side + 1) * half, :] = own_held[1 - side].T
    fetched.update({p: fetch(p) for p in range(1, min(depth, count))})
    sent = {}
    for p in range(count):
        for copy in fetched[p]:
            copy.wait()
        if p >= 2:
            sent[p - 2].wait()
        for side in range(2):
            total = jnp.dot(
                turned[...], held[p % depth, 1 - side], preferred_element_type=jnp.float32
            )
            result[p % 2, :, side * half : (side + 1) * half] = total * scale_ref[0]
        if p + depth < count:
            fetched[p + depth] = fetch(p + depth)
        cols = pl.ds(pl.multiple_of(ids_ref[start + p] * 2 * half, 2 * half), 2 * half)
        sent[p] = pltpu.make_async_copy(result.at[p % 2], out_ref.at[:, cols], out_sems.at[p % 2])
        sent[p].start()
    for p in range(max(0, count - 2), count):
        sent[p].wait()


def gram(ids, start, scale, own, pairs, features, token, old=None):
    arrays, sources, rows = indexed(pairs)
    half = arrays[0].shape[2]
    first = own.ndim == 3
    extra = 1 if old is None else 2
    turned = ((2 * half, rows), jnp.bfloat16)
    return pl.pallas_call(
        functools.partial(gram_kernel, sources, start, len(arrays), first, extra),
        out_shape=(
            jax.ShapeDtypeStruct((2 * half, features), jnp.float32),
            jax.ShapeDtypeStruct((8, 128), jnp.float32),
        )
        + ((jax.ShapeDtypeStruct(*turned),) if first else ()),
        in_specs=[SMEM] * 2 + [ANY] * (1 + len(arrays) + extra),
        out_specs=(ANY, VMEM) + ((VMEM,) if first else ()),
        scratch_shapes=[
            pltpu.VMEM((2, rows, half), jnp.bfloat16) if first else pltpu.VMEM(*turned),
            pltpu.VMEM((3, 2, rows, half), jnp.bfloat16),
            pltpu.VMEM((2, 2 * half, 2 * half), jnp.float32),
            pltpu.SemaphoreType.DMA(()),
            pltpu.SemaphoreType.DMA((3, 2)),
            pltpu.SemaphoreType.DMA((2,)),
        ],
        input_output_aliases={} if old is None else {4 + len(arrays): 0},
        compiler_params=pltpu.CompilerParams(vmem_limit_bytes=VMEM_BYTES),
        cost_estimate=cost(1),
        interpret=INTERPRET,
    )(ids, scale, own, *arrays, token, *([] if old is None else [old]))


class Spread:
    def __init__(self):
        self.found = {}

    def keep(self, arrays, at, dl, core):
        twins = [swap(array, "c") for array in arrays]
        at_twin = {"o": "o", "m": "p", "f": "f"}[at]
        self.found[at, dl, core] = arrays
        self.found[at_twin, dl, 1 - core] = twins
        return twins

    def open(self, pair, twin=None):
        beside, near = swap(pair, "l"), ring_hop(pair, "x")
        if twin is None:
            twin = swap(pair, "c")
        near_twin = ring_hop(twin, "x")
        self.found["o", 0, 0], self.found["o", 0, 1] = [pair], [twin]
        self.moved = (beside, near, near_twin)

    def first(self, token):
        beside, near, near_twin = self.moved
        near, token = tie(near, token)
        near_beside, far = swap(near, "l"), ring_hop(near, "x")
        beside, near_twin, token = lax.optimization_barrier((beside, near_twin, token))
        (twin,) = self.keep([beside], "o", 1, 0)
        beside_near = ring_hop(twin, "x")
        self.keep([near], "m", 0, 0)
        self.keep([near_twin], "m", 0, 1)
        self.moved = (far, near_beside, beside_near)
        return token

    def third(self, token):
        far, near_beside, beside_near = self.moved
        far, token = tie(far, token)
        rows = far.shape[1] // 3
        over_l = swap(far[:, :rows], "l")
        near_beside, token = tie(near_beside, token)
        over_x = ring_hop(near_beside[:, rows:], "x")
        self.keep([near_beside], "m", 1, 0)
        beside_near, token = tie(beside_near, token)
        self.keep([beside_near], "m", 1, 1)
        self.keep([far], "f", 0, 0)
        self.moved = (over_l, over_x)
        return token

    def end(self, token):
        *moved, token = lax.optimization_barrier((*self.moved, token))
        self.keep(moved, "f", 1, 0)
        return token


def local(tokens, routes, counts, gate_weight, up_weight):
    x, l, c = lax.axis_index("x"), lax.axis_index("l"), lax.axis_index("c")
    expert = lax.axis_index("y") * 2 + lax.axis_index("h")
    gate_panel, up_panel = gate_weight[0], up_weight[0]
    width, panel = gate_panel.shape
    features = 16 * panel
    routed_total = jnp.sum(jnp.where(jnp.arange(8) == expert, counts, 0)).astype(jnp.float32)
    scale = (2.0 / routed_total).reshape(1)
    expert = expert.reshape(1).astype(jnp.int32)

    tagged = jnp.concatenate(
        [tokens, jnp.pad(routes.astype(tokens.dtype), ((0, 0), (0, ROUTE_LANES - 2)))], axis=1
    )
    pair = jnp.stack([tagged, far_swap(tagged)])
    near, back = ring_hop(pair, "y"), ring_back(pair, "y")
    far = lax.ppermute(pair, "y", [(i, (i + 2) % 4) for i in range(4)])
    parts = [(a, swap(a, "c")) for a in (pair, near, back, far)]

    block = 8 * SLOTS
    y_near, y_back = 1 + c, 2 - c
    base = []
    for y_mine, y_twin in ((0, 0), (y_near, y_back), (y_back, y_near), (3, 3)):
        for dc, y_of in ((0, y_mine), (1, y_twin)):
            base += [dc * block + (2 * y_of + dh) * SLOTS for dh in (0, 1)]
    base = jnp.stack([jnp.asarray(b, jnp.int32) for b in base])
    base = jnp.broadcast_to(jnp.repeat(base, 16).astype(jnp.float32), (8, 256))
    blocks = [a.reshape((-1, a.shape[-1])) for part in parts for a in part]
    pair, twin = select(expert, base, blocks, width)

    place_of = {"o": x, "m": x - (1 - 2 * c), "p": x + (1 - 2 * c), "f": x + 2}

    def chip(at, dl):
        return (place_of[at] % 4) * 2 + (l + dl) % 2

    chips_all = [("o", 0), ("o", 1), ("m", 0), ("p", 0), ("m", 1), ("p", 1), ("f", 0), ("f", 1)]
    ids = [chip(at, dl) * 2 + (c + core) % 2 for at, dl in chips_all for core in (0, 1)]
    ids = jnp.stack(ids).astype(jnp.int32)
    offsets = ids * block

    def place_in(chips):
        return 2 * chips_all.index(chips[0])

    def blocks_of(spread, chips):
        return [spread.found[at, dl, core] for at, dl in chips for core in (0, 1)]

    total = 16 * block

    def hidden_of(chips, token, *old):
        found = blocks_of(rows, chips)
        return ffn(offsets, place_in(chips), found, gate_panel, up_panel, total, token, old)

    token = jnp.zeros((8, 128), jnp.float32)
    rows = Spread()
    rows.open(pair, twin)
    hidden, token = hidden_of([("o", 0)], token)
    token = rows.first(token)
    hidden, token = hidden_of([("o", 1), ("m", 0), ("p", 0)], token, hidden)
    token = rows.third(token)
    hidden, token = hidden_of([("m", 1), ("p", 1), ("f", 0)], token, hidden)
    token = rows.end(token)
    hidden, token = hidden_of([("f", 1)], token, hidden)

    def part(chips, token, old=None):
        found = blocks_of(panels, chips)
        return gram(ids, place_in(chips), scale, own, found, features, token, old)

    panels = Spread()
    panels.open(hidden)
    token = panels.first(token)
    own = hidden
    out, token, own = part([("o", 0), ("o", 1), ("m", 0), ("p", 0)], token)
    token = panels.third(token)
    out, token = part([("m", 1), ("p", 1), ("f", 0)], token, out)
    token = panels.end(token)
    out, token = part([("f", 1)], token, out)
    return out[None]


def solution(mesh):
    fine = Mesh(mesh.devices.reshape(4, 2, 4, 2, 2), AXES)
    rows = P(AXES, None)
    weight = P(("y", "h"), None, ("x", "l", "c"))
    return jax.shard_map(
        local,
        mesh=fine,
        in_specs=(rows, rows, P(), weight, weight),
        out_specs=P(("y", "h"), ("x", "l", "c"), None),
        check_vma=False,
    )
```

```python
import functools

import jax
import jax.numpy as jnp
from jax import lax
from jax.experimental import pallas as pl
from jax.experimental.pallas import tpu as pltpu
from jax.sharding import Mesh
from jax.sharding import PartitionSpec as P

AXES = ("y", "h", "x", "l", "c")
ROUTE_LANES = 128
VMEM_BYTES = 56 * 1024 * 1024
SLOTS = 12
INTERPRET = False
ANY = pl.BlockSpec(memory_space=pl.ANY)
SMEM = pl.BlockSpec(memory_space=pltpu.SMEM)
VMEM = pl.BlockSpec(memory_space=pltpu.VMEM)


def ring_hop(a, axis):
    pairs = [(2 * i + c, 2 * ((i + (1, 3)[c]) % 4) + c) for i in range(4) for c in range(2)]
    return lax.ppermute(a, (axis, "c"), pairs)


def ring_back(a, axis):
    pairs = [(2 * i + c, 2 * ((i + (3, 1)[c]) % 4) + c) for i in range(4) for c in range(2)]
    return lax.ppermute(a, (axis, "c"), pairs)


def swap(a, axis):
    return lax.ppermute(a, axis, [(0, 1), (1, 0)])


def far_swap(a):
    return lax.ppermute(a, ("h", "l"), [(0, 3), (3, 0), (1, 2), (2, 1)])


def after(a, *others):
    return lax.optimization_barrier((a,) + others)[0]


def tie(a, token):
    return lax.optimization_barrier((a, token))


def cost(microseconds):
    return pl.CostEstimate(
        flops=int(microseconds * 1_150_000_000), bytes_accessed=1_000_000, transcendentals=0
    )


def select_kernel(n, width, expert_ref, base_ref, *rest):
    sources, (own_ref, twin_ref, held, sems) = rest[:n], rest[n:]
    copies, row = [], 0
    for i, source in enumerate(sources):
        rows = pl.ds(row, source.shape[0])
        copies.append(pltpu.make_async_copy(source, held.at[rows], sems.at[i]))
        copies[-1].start()
        row += source.shape[0]
    tokens, out_rows = held.shape[0], 2 * own_ref.shape[1]
    first = lax.broadcasted_iota(jnp.int32, (tokens, tokens), 0)
    second = lax.broadcasted_iota(jnp.int32, (tokens, tokens), 1)
    earlier = jnp.logical_and(first // 16 == second // 16, first < second)
    earlier = earlier.astype(jnp.float32).astype(jnp.bfloat16)
    lane = lax.broadcasted_iota(jnp.int32, (tokens, ROUTE_LANES), 1)
    places = lax.broadcasted_iota(jnp.int32, (out_rows, tokens), 0).astype(jnp.float32)
    ones = jnp.ones((16, ROUTE_LANES), jnp.bfloat16)
    for copy in copies:
        copy.wait()
    named = held[:, width:].astype(jnp.float32) == expert_ref[0].astype(jnp.float32)
    named = jnp.logical_and(named, lane < 2).astype(jnp.float32).astype(jnp.bfloat16)
    named = lax.dot_general(
        ones, named, (((1,), (1,)), ((), ())), preferred_element_type=jnp.float32
    )
    rank = jnp.dot(named.astype(jnp.bfloat16), earlier, preferred_element_type=jnp.float32)
    place = jnp.where(named[0:1, :] > 0.5, base_ref[0:1, :] + rank[0:1, :], -1.0)
    pick = (places == place).astype(jnp.float32).astype(jnp.bfloat16)
    half = width // 2
    for side, start in ((0, half), (1, 0)):
        got = jnp.dot(pick, held[:, start : start + half], preferred_element_type=jnp.float32)
        got = got.astype(jnp.bfloat16)
        own_ref[side] = got[: out_rows // 2]
        twin_ref[side] = got[out_rows // 2 :]


def select(expert, base, blocks, width):
    tokens = sum(b.shape[0] for b in blocks)
    half = jax.ShapeDtypeStruct((2, tokens // 32 * SLOTS, width // 2), jnp.bfloat16)
    return pl.pallas_call(
        functools.partial(select_kernel, len(blocks), width),
        out_shape=(half, half),
        in_specs=[SMEM, VMEM] + [ANY] * len(blocks),
        out_specs=(VMEM, VMEM),
        scratch_shapes=[
            pltpu.VMEM((tokens, blocks[0].shape[1]), jnp.bfloat16),
            pltpu.SemaphoreType.DMA((len(blocks),)),
        ],
        compiler_params=pltpu.CompilerParams(vmem_limit_bytes=VMEM_BYTES),
        cost_estimate=cost(3),
        interpret=INTERPRET,
    )(expert, base, *blocks)


def ffn_kernel(blocks, first, n_arrays, n_old, offsets_ref, *rest):
    arrays, (gate_hbm, up_hbm) = rest[:n_arrays], rest[n_arrays : n_arrays + 2]
    (
        out_ref,
        token_ref,
        rows,
        gate_held,
        up_held,
        result,
        sems,
        weight_sems,
        out_sems,
    ) = rest[n_arrays + 2 + n_old :]
    token_ref[...] = jnp.zeros_like(token_ref)
    piece_rows = rows.shape[0] // len(blocks)
    width, half = rows.shape[1] // 2, gate_held.shape[1] // 2
    copies = []
    for i, parts in enumerate(blocks):
        for array, start, count in parts:
            for side in range(2):
                target = rows.at[
                    pl.ds(i * piece_rows + start, count), pl.ds(side * width, width)
                ]
                copies.append(
                    pltpu.make_async_copy(
                        arrays[array].at[1 - side], target, sems.at[len(copies)]
                    )
                )
    weight_copies = []
    for q in range(2):
        cols = pl.ds(q * half, half)
        for j, (src, dst) in enumerate(((gate_hbm, gate_held), (up_hbm, up_held))):
            weight_copies.append(
                pltpu.make_async_copy(src.at[:, cols], dst.at[:, cols], weight_sems.at[2 * q + j])
            )
    late = weight_copies[2:] if len(blocks) > 2 else []
    for copy in weight_copies[:2] + copies + ([] if late else weight_copies[2:]):
        copy.start()
    for copy in copies:
        copy.wait()
    sent = []
    for q in range(2):
        weight_copies[2 * q].wait()
        weight_copies[2 * q + 1].wait()
        if q == 0:
            for copy in late:
                copy.start()
        cols = slice(q * half, (q + 1) * half)
        gate = jnp.dot(rows[...], gate_held[:, cols], preferred_element_type=jnp.float32)
        up = jnp.dot(rows[...], up_held[:, cols], preferred_element_type=jnp.float32)
        result[q] = (gate / (1.0 + jnp.exp(-gate)) * up).astype(jnp.bfloat16)
        for i in range(len(blocks)):
            to = pl.ds(pl.multiple_of(offsets_ref[first + i], 16), piece_rows)
            sent.append(
                pltpu.make_async_copy(
                    result.at[q, pl.ds(i * piece_rows, piece_rows)],
                    out_ref.at[1 - q, to],
                    out_sems.at[q, i],
                )
            )
            sent[-1].start()
    for copy in sent:
        copy.wait()


def indexed(blocks):
    arrays, sources = [], []
    for parts in blocks:
        sources.append([])
        start = 0
        for array in parts:
            at = [i for i, known in enumerate(arrays) if known is array]
            if not at:
                arrays.append(array)
                at = [len(arrays) - 1]
            sources[-1].append((at[0], start, array.shape[1]))
            start += array.shape[1]
    return arrays, sources, start


def ffn(offsets, first, blocks, wg, wu, total_rows, token, old=()):
    arrays, sources, piece_rows = indexed(blocks)
    width, panel = wg.shape
    rows = len(blocks) * piece_rows
    out = jax.ShapeDtypeStruct((2, total_rows, panel // 2), jnp.bfloat16)
    first_old = 4 + len(arrays)
    return pl.pallas_call(
        functools.partial(ffn_kernel, sources, first, len(arrays), len(old) + 1),
        out_shape=(out, jax.ShapeDtypeStruct((8, 128), jnp.float32)),
        in_specs=[SMEM] + [ANY] * (len(arrays) + 3 + len(old)),
        out_specs=(ANY, VMEM),
        scratch_shapes=[
            pltpu.VMEM((rows, width), jnp.bfloat16),
            pltpu.VMEM(wg.shape, jnp.bfloat16),
            pltpu.VMEM(wu.shape, jnp.bfloat16),
            pltpu.VMEM((2, rows, panel // 2), jnp.bfloat16),
            pltpu.SemaphoreType.DMA((2 * sum(len(parts) for parts in sources),)),
            pltpu.SemaphoreType.DMA((4,)),
            pltpu.SemaphoreType.DMA((2, len(blocks))),
        ],
        input_output_aliases={first_old + i: i for i in range(len(old))},
        compiler_params=pltpu.CompilerParams(vmem_limit_bytes=VMEM_BYTES),
        cost_estimate=cost(1),
        interpret=INTERPRET,
    )(offsets, *arrays, wg, wu, token, *old)


def gram_kernel(sources, start, n_arrays, first, extra, ids_ref, scale_ref, *rest):
    own_ref, *arrays = rest[: 1 + n_arrays]
    out_ref, token_ref, *rest = rest[1 + n_arrays + extra :]
    if first:
        turned, own_held, held, result, own_sem, in_sems, out_sems = rest
    else:
        turned, held, result, own_sem, in_sems, out_sems = rest
    token_ref[...] = jnp.zeros_like(token_ref)
    half = held.shape[3]
    depth, count = held.shape[0], len(sources)

    def fetch(p):
        copies = []
        for k, (array, row, rows) in enumerate(sources[p]):
            target = held.at[p % depth, :, pl.ds(row, rows)]
            copies.append(pltpu.make_async_copy(arrays[array], target, in_sems.at[p % depth, k]))
            copies[-1].start()
        return copies

    own = pltpu.make_async_copy(own_ref, own_held if first else turned, own_sem)
    own.start()
    fetched = {0: fetch(0)}
    own.wait()
    if first:
        for side in range(2):
            turned[side * half : (side + 1) * half, :] = own_held[1 - side].T
    fetched.update({p: fetch(p) for p in range(1, min(depth, count))})
    sent = {}
    for p in range(count):
        for copy in fetched[p]:
            copy.wait()
        if p >= 2:
            sent[p - 2].wait()
        for side in range(2):
            total = jnp.dot(
                turned[...], held[p % depth, 1 - side], preferred_element_type=jnp.float32
            )
            result[p % 2, :, side * half : (side + 1) * half] = total * scale_ref[0]
        if p + depth < count:
            fetched[p + depth] = fetch(p + depth)
        cols = pl.ds(pl.multiple_of(ids_ref[start + p] * 2 * half, 2 * half), 2 * half)
        sent[p] = pltpu.make_async_copy(result.at[p % 2], out_ref.at[:, cols], out_sems.at[p % 2])
        sent[p].start()
    for p in range(max(0, count - 2), count):
        sent[p].wait()


def gram(ids, start, scale, own, pairs, features, token, old=None):
    arrays, sources, rows = indexed(pairs)
    half = arrays[0].shape[2]
    first = own.ndim == 3
    extra = 1 if old is None else 2
    turned = ((2 * half, rows), jnp.bfloat16)
    return pl.pallas_call(
        functools.partial(gram_kernel, sources, start, len(arrays), first, extra),
        out_shape=(
            jax.ShapeDtypeStruct((2 * half, features), jnp.float32),
            jax.ShapeDtypeStruct((8, 128), jnp.float32),
        )
        + ((jax.ShapeDtypeStruct(*turned),) if first else ()),
        in_specs=[SMEM] * 2 + [ANY] * (1 + len(arrays) + extra),
        out_specs=(ANY, VMEM) + ((VMEM,) if first else ()),
        scratch_shapes=[
            pltpu.VMEM((2, rows, half), jnp.bfloat16) if first else pltpu.VMEM(*turned),
            pltpu.VMEM((3, 2, rows, half), jnp.bfloat16),
            pltpu.VMEM((2, 2 * half, 2 * half), jnp.float32),
            pltpu.SemaphoreType.DMA(()),
            pltpu.SemaphoreType.DMA((3, 2)),
            pltpu.SemaphoreType.DMA((2,)),
        ],
        input_output_aliases={} if old is None else {4 + len(arrays): 0},
        compiler_params=pltpu.CompilerParams(vmem_limit_bytes=VMEM_BYTES),
        cost_estimate=cost(1),
        interpret=INTERPRET,
    )(ids, scale, own, *arrays, token, *([] if old is None else [old]))


class Spread:
    def __init__(self, share):
        self.found, self.share = {}, share

    def keep(self, arrays, at, dl, core):
        twins = [swap(array, "c") for array in arrays]
        at_twin = {"o": "o", "m": "p", "f": "f"}[at]
        self.found[at, dl, core] = arrays
        self.found[at_twin, dl, 1 - core] = twins
        return twins

    def open(self, pair, twin=None):
        beside, near = swap(pair, "l"), ring_hop(pair, "x")
        if twin is None:
            twin = swap(pair, "c")
        near_twin = ring_hop(twin, "x")
        self.found["o", 0, 0], self.found["o", 0, 1] = [pair], [twin]
        self.moved = (beside, near, near_twin)

    def first(self, token):
        beside, near, near_twin = self.moved
        near, token = tie(near, token)
        near_beside, far = swap(near, "l"), ring_hop(near, "x")
        beside, near_twin, token = lax.optimization_barrier((beside, near_twin, token))
        (twin,) = self.keep([beside], "o", 1, 0)
        beside_near = ring_hop(twin, "x")
        self.keep([near], "m", 0, 0)
        self.keep([near_twin], "m", 0, 1)
        self.moved = (far, near_beside, beside_near)
        return token

    def third(self, token):
        far, near_beside, beside_near = self.moved
        far, token = tie(far, token)
        rows = far.shape[1] // self.share if self.share else 0
        over_l = (swap(far[:, :rows], "l"),) if rows else ()
        near_beside, token = tie(near_beside, token)
        over_x = ring_hop(near_beside[:, rows:] if rows else near_beside, "x")
        self.keep([near_beside], "m", 1, 0)
        beside_near, token = tie(beside_near, token)
        self.keep([beside_near], "m", 1, 1)
        self.keep([far], "f", 0, 0)
        self.moved = over_l + (over_x,)
        return token

    def end(self, token):
        *moved, token = lax.optimization_barrier((*self.moved, token))
        self.keep(moved, "f", 1, 0)
        return token


def local(tokens, routes, counts, gate_weight, up_weight):
    x, l, c = lax.axis_index("x"), lax.axis_index("l"), lax.axis_index("c")
    expert = lax.axis_index("y") * 2 + lax.axis_index("h")
    gate_panel, up_panel = gate_weight[0], up_weight[0]
    width, panel = gate_panel.shape
    features = 16 * panel
    routed_total = jnp.sum(jnp.where(jnp.arange(8) == expert, counts, 0)).astype(jnp.float32)
    scale = (2.0 / routed_total).reshape(1)
    expert = expert.reshape(1).astype(jnp.int32)

    tagged = jnp.concatenate(
        [tokens, jnp.pad(routes.astype(tokens.dtype), ((0, 0), (0, ROUTE_LANES - 2)))], axis=1
    )
    pair = jnp.stack([tagged, far_swap(tagged)])
    near, back = ring_hop(pair, "y"), ring_back(pair, "y")
    far = lax.ppermute(pair, "y", [(i, (i + 2) % 4) for i in range(4)])
    parts = [(a, swap(a, "c")) for a in (pair, near, back, far)]

    block = 8 * SLOTS
    y_near, y_back = 1 + c, 2 - c
    base = []
    for y_mine, y_twin in ((0, 0), (y_near, y_back), (y_back, y_near), (3, 3)):
        for dc, y_of in ((0, y_mine), (1, y_twin)):
            base += [dc * block + (2 * y_of + dh) * SLOTS for dh in (0, 1)]
    base = jnp.stack([jnp.asarray(b, jnp.int32) for b in base])
    base = jnp.broadcast_to(jnp.repeat(base, 16).astype(jnp.float32), (8, 256))
    blocks = [a.reshape((-1, a.shape[-1])) for part in parts for a in part]
    pair, twin = select(expert, base, blocks, width)

    place_of = {"o": x, "m": x - (1 - 2 * c), "p": x + (1 - 2 * c), "f": x + 2}

    def chip(at, dl):
        return (place_of[at] % 4) * 2 + (l + dl) % 2

    chips_all = [("o", 0), ("o", 1), ("m", 0), ("p", 0), ("m", 1), ("p", 1), ("f", 0), ("f", 1)]
    ids = [chip(at, dl) * 2 + (c + core) % 2 for at, dl in chips_all for core in (0, 1)]
    ids = jnp.stack(ids).astype(jnp.int32)
    offsets = ids * block

    def place_in(chips):
        return 2 * chips_all.index(chips[0])

    def blocks_of(spread, chips):
        return [spread.found[at, dl, core] for at, dl in chips for core in (0, 1)]

    total = 16 * block

    def hidden_of(chips, token, *old):
        found = blocks_of(rows, chips)
        return ffn(offsets, place_in(chips), found, gate_panel, up_panel, total, token, old)

    token = jnp.zeros((8, 128), jnp.float32)
    rows = Spread(0)
    rows.open(pair, twin)
    hidden, token = hidden_of([("o", 0)], token)
    token = rows.first(token)
    hidden, token = hidden_of([("o", 1), ("m", 0), ("p", 0)], token, hidden)
    token = rows.third(token)
    hidden, token = hidden_of([("m", 1), ("p", 1), ("f", 0)], token, hidden)
    token = rows.end(token)
    hidden, token = hidden_of([("f", 1)], token, hidden)

    def part(chips, token, old=None):
        found = blocks_of(panels, chips)
        return gram(ids, place_in(chips), scale, own, found, features, token, old)

    panels = Spread(3)
    panels.open(hidden)
    token = panels.first(token)
    own = hidden
    out, token, own = part([("o", 0), ("o", 1), ("m", 0), ("p", 0)], token)
    token = panels.third(token)
    out, token = part([("m", 1), ("p", 1), ("f", 0)], token, out)
    token = panels.end(token)
    out, token = part([("f", 1)], token, out)
    return out[None]


def solution(mesh):
    fine = Mesh(mesh.devices.reshape(4, 2, 4, 2, 2), AXES)
    rows = P(AXES, None)
    weight = P(("y", "h"), None, ("x", "l", "c"))
    return jax.shard_map(
        local,
        mesh=fine,
        in_specs=(rows, rows, P(), weight, weight),
        out_specs=P(("y", "h"), ("x", "l", "c"), None),
        check_vma=False,
    )
```
